256 devices in a mesh: dp: 16 (over x_lo, y, core), dap: 16 (over z, x_hi).
Axes of the slice: x: 4 (x_hi: 2, x_lo: 2; x = x_hi * 2 + x_lo), y: 4, z: 8, core: 2. Of those that a mesh axis runs over, the one named last changes fastest.
Arguments:
- symbol_codes: int32 [16, 128, 256], P('dp', None, 'dap'), may hold values from 0 to 22
- aligned_validity: int32 [16, 128, 256], P('dp', None, 'dap'), may hold values 0 or 1
- pair_update_cotangent: bfloat16 [16, 256, 256, 128], P('dp', 'dap'), may hold values from -6 to 6
- aligned_feature_adjoint: bfloat16 [16, 128, 256, 256], P('dp', None, 'dap'), may hold values from -6 to 6
- local_master_weights: float32 [154048], replicated, as said below
- local_first_moment: float32 [154048], replicated, as said below
- local_second_moment: float32 [154048], replicated, as said below
- remaining_master_weights: float32 [65536, 512], P(('dp', 'dap')), may hold values from -0.875 to 0.875
- remaining_first_moment: float32 [65536, 512], P(('dp', 'dap')), as said below
- remaining_second_moment: float32 [65536, 512], P(('dp', 'dap')), as said below
- remaining_gradient: float32 [65536, 512], P(('dp', 'dap'))
Outputs:
- new_window_master: float32 [154048], replicated
- new_window_mom1: float32 [154048], replicated
- new_window_mom2: float32 [154048], replicated
- window_copy: bfloat16 [154048], replicated
- new_rest_master: float32 [65536, 512], P(('dp', 'dap'))
- new_rest_mom1: float32 [65536, 512], P(('dp', 'dap'))
- new_rest_mom2: float32 [65536, 512], P(('dp', 'dap'))
- rest_copy: bfloat16 [65536, 512], P(('dp', 'dap'))
The draws below stay inside these ranges and needn't reach their ends.
Inputs may be any that keep to these rules, and one draw needn't show every extreme that they name: `local_master_weights`: float32 masters in the order of weights. `local_first_moment`: first moments. `local_second_moment`: second moments, positive. `remaining_first_moment`: first moments. `remaining_second_moment`: second moments, positive.
All inputs are finite; a program needn't handle non-finite values. No bound on the sum of `aligned_validity` on one device may be relied on, other than what follows from the above.
Results may differ from the reference program's by a relative error of at most 0.0049.
Values may be sent and summed in bfloat16 or wider, within the bound.
A program may use at most 192 MiB of HBM per device.

```python
import math
import jax
import jax.numpy as jnp
from jax import lax

FEATURE_WIDTH = 256
COUPLING_WIDTH = 128
OUTER_LATENT = 32
SYMBOL_KINDS = 23
HOMOLOG_DEPTH = 128
RES_DEV = 16
COLS = 512
STEP = 10
SAMPLE_WINDOWS = 16
PEPTIDE_LENGTH = 256
ROWS = 65536
PARAM_TOTAL = 154048
N_DAP = 16


def window_blocks():
    retained_fraction = 0.875
    activation_factor = math.sqrt(retained_fraction * PEPTIDE_LENGTH * COUPLING_WIDTH / OUTER_LATENT) / HOMOLOG_DEPTH
    magnitude_factor = activation_factor * math.sqrt(retained_fraction * 2 * OUTER_LATENT / FEATURE_WIDTH)
    locations_list = SAMPLE_WINDOWS * HOMOLOG_DEPTH * PEPTIDE_LENGTH
    coupled_couples = SAMPLE_WINDOWS * PEPTIDE_LENGTH * PEPTIDE_LENGTH
    active_flags = math.sqrt(locations_list * retained_fraction)
    lookup_multiplier = math.sqrt(locations_list / SYMBOL_KINDS) * math.sqrt(0.25 + SYMBOL_KINDS * magnitude_factor * magnitude_factor)
    segment_groups = [(FEATURE_WIDTH, active_flags * magnitude_factor), (FEATURE_WIDTH, active_flags * magnitude_factor), (FEATURE_WIDTH * 2 * OUTER_LATENT, active_flags * activation_factor), (2 * OUTER_LATENT, active_flags * activation_factor), (OUTER_LATENT * OUTER_LATENT * COUPLING_WIDTH, math.sqrt(coupled_couples) * retained_fraction / math.sqrt(HOMOLOG_DEPTH)), (COUPLING_WIDTH, math.sqrt(coupled_couples)), (SYMBOL_KINDS * FEATURE_WIDTH, lookup_multiplier)]
    squares = 0.0
    for amount, magnitude in segment_groups:
        squares = squares + amount * magnitude * magnitude
    return (segment_groups, squares)


def window_rates():
    segment_groups, squares = window_blocks()
    whole = math.sqrt(2.0 * squares)
    return jnp.concatenate([jnp.full((amount,), 0.1 * magnitude / whole, jnp.float32) for amount, magnitude in segment_groups])


def spread_mean():
    return 99.0 / (2.0 * math.log(10.0))


def rise_mean(rise_log):
    return (math.exp(2.0 * rise_log) - 1.0) / (2.0 * rise_log)


def rest_factors(key, rise_log):
    key = jax.random.fold_in(key, 101)
    key_rows, key_cols = jax.random.split(key)
    position = jnp.arange(ROWS, dtype=jnp.float32)[:, None] / ROWS
    row_scale = jnp.exp(jax.random.uniform(key_rows, (ROWS, 1), jnp.float32) * math.log(10.0))
    col_scale = jnp.exp(jax.random.uniform(key_cols, (1, COLS), jnp.float32) * math.log(10.0))
    rising = jnp.exp(position * rise_log)
    return row_scale * col_scale * rising


def rest_rates(key, rise_log):
    factors = rest_factors(key, rise_log)
    whole = math.sqrt(2.0 * ROWS * COLS * spread_mean() * spread_mean() * rise_mean(rise_log))
    return 0.1 * factors / whole


def draw_local_master_weights(key, part):
    key = jax.random.fold_in(key, 5)
    deviation_values = [(FEATURE_WIDTH, 0.1), (FEATURE_WIDTH, 0.1), (FEATURE_WIDTH * 2 * OUTER_LATENT, 1.0 / math.sqrt(FEATURE_WIDTH)), (2 * OUTER_LATENT, 0.1), (OUTER_LATENT * OUTER_LATENT * COUPLING_WIDTH, 1.0 / OUTER_LATENT), (COUPLING_WIDTH, 0.1), (SYMBOL_KINDS * FEATURE_WIDTH, 1.0 / math.sqrt(SYMBOL_KINDS))]
    scales = jnp.concatenate([jnp.full((amount,), spread, jnp.float32) for amount, spread in deviation_values])
    starting_shifts = jnp.concatenate([jnp.ones((FEATURE_WIDTH,), jnp.float32), jnp.zeros((PARAM_TOTAL - FEATURE_WIDTH,), jnp.float32)])
    noise = jax.random.normal(key, (PARAM_TOTAL,), jnp.float32)
    return (starting_shifts + scales * noise).astype(jnp.float32)


def draw_local_first_moment(key, part):
    key = jax.random.fold_in(key, 6)
    rates = window_rates()
    noise = jax.random.normal(key, (PARAM_TOTAL,), jnp.float32)
    return (0.3 * rates * noise).astype(jnp.float32)


def draw_local_second_moment(key, part):
    key = jax.random.fold_in(key, 7)
    rates = window_rates()
    spread = jax.random.uniform(key, (PARAM_TOTAL,), jnp.float32, -0.7, 0.7)
    return (0.01 * rates * rates * jnp.exp(spread)).astype(jnp.float32)


def draw_remaining_gradient(key, part):
    rise_log = math.log(3.0)
    factors = rest_factors(key, rise_log)
    key = jax.random.fold_in(key, 11)
    key_base = jax.random.fold_in(key, 0)
    base = jax.random.normal(key_base, (ROWS, COLS), jnp.float32)
    segment_groups, squares = window_blocks()
    amplitude = math.sqrt(squares / (ROWS * COLS * spread_mean() * spread_mean() * rise_mean(rise_log)))
    return (amplitude * base * factors).astype(jnp.float32)


def draw_remaining_first_moment(key, part):
    rise_log = math.log(3.0)
    rates = rest_rates(key, rise_log)
    key = jax.random.fold_in(key, 12)
    noise = jax.random.normal(key, (ROWS, COLS), jnp.float32)
    return (0.3 * rates * noise).astype(jnp.float32)


def draw_remaining_second_moment(key, part):
    rise_log = math.log(3.0)
    rates = rest_rates(key, rise_log)
    key = jax.random.fold_in(key, 13)
    spread = jax.random.uniform(key, (ROWS, COLS), jnp.float32, -0.7, 0.7)
    return (0.01 * rates * rates * jnp.exp(spread)).astype(jnp.float32)


def plant(values, key, least, high):
    longest = values.shape.index(max(values.shape))
    spots = []
    for shift in (0, 1):
        where = [jax.random.randint(jax.random.fold_in(key, axis), (), 0, length) for axis, length in enumerate(values.shape)]
        where[longest] = (where[longest] + shift) % values.shape[longest]
        spots.append(tuple(where))
    return values.at[spots[0]].set(least).at[spots[1]].set(high)


def steps_of(stream_key, dims, cuts, low, top_value):
    level, own = 1.0, jax.random.fold_in(stream_key, 6)
    for dim, parts in cuts:
        steps = jnp.exp(jax.random.uniform(jax.random.fold_in(own, dim), (parts,), jnp.float32, low / len(cuts), top_value / len(cuts)))
        level = level * jnp.repeat(steps, dims[dim] // parts).reshape([-1 if axis == dim else 1 for axis in range(len(dims))])
    return level


def bell_draw(own_key, shape, scale, bound, cuts=(), kind=jnp.bfloat16):
    drawn = jax.random.normal(own_key, shape, jnp.float32) * scale
    if len(cuts) > 0:
        drawn = steps_of(own_key, shape, cuts, -0.22, 0.18) * drawn
    return jnp.clip(drawn, min=-bound, max=bound).astype(kind)


def setup_inputs(seed: int = 0) -> dict:
    key_list = jax.random.split(jax.random.key(seed), 12)
    return {
        "symbol_codes": plant(jax.random.randint(key_list[0], (SAMPLE_WINDOWS, HOMOLOG_DEPTH, PEPTIDE_LENGTH), 0, SYMBOL_KINDS), jax.random.fold_in(key_list[0], 1), 0, SYMBOL_KINDS - 1).astype(jnp.int32),
        "aligned_validity": plant((jax.random.randint(key_list[1], (SAMPLE_WINDOWS, HOMOLOG_DEPTH, PEPTIDE_LENGTH), 0, 8) < 7).astype(jnp.int32), jax.random.fold_in(key_list[1], 1), 0, 1),
        "pair_update_cotangent": bell_draw(key_list[2], (SAMPLE_WINDOWS, PEPTIDE_LENGTH, PEPTIDE_LENGTH, COUPLING_WIDTH), 1.0, 6.0, ((0, 16), (1, 16))),
        "aligned_feature_adjoint": bell_draw(key_list[3], (SAMPLE_WINDOWS, HOMOLOG_DEPTH, PEPTIDE_LENGTH, FEATURE_WIDTH), 0.5, 6.0, ((0, 16), (2, 16))),
        "local_master_weights": draw_local_master_weights(jax.random.fold_in(key_list[11], 71), 0),
        "local_first_moment": draw_local_first_moment(jax.random.fold_in(key_list[11], 71), 0),
        "local_second_moment": draw_local_second_moment(jax.random.fold_in(key_list[11], 71), 0),
        "remaining_master_weights": bell_draw(key_list[7], (ROWS, COLS), 0.06, 0.875, ((0, 256),), jnp.float32),
        "remaining_first_moment": draw_remaining_first_moment(jax.random.fold_in(key_list[11], 71), 0),
        "remaining_second_moment": draw_remaining_second_moment(jax.random.fold_in(key_list[11], 71), 0),
        "remaining_gradient": draw_remaining_gradient(jax.random.fold_in(key_list[11], 71), 0),
    }


beta_first = 0.9
beta_second = 0.999
adam_eps = 1e-06
learn_rate = 0.001
clip_norm = 0.1
norm_eps = 1e-05

def unpack(vector):
    segment_extents = [FEATURE_WIDTH, FEATURE_WIDTH, FEATURE_WIDTH * 2 * OUTER_LATENT, 2 * OUTER_LATENT, OUTER_LATENT * OUTER_LATENT * COUPLING_WIDTH, COUPLING_WIDTH, SYMBOL_KINDS * FEATURE_WIDTH]
    fragment_parts = []
    offset = 0
    for length in segment_extents:
        fragment_parts.append(vector[offset:offset + length])
        offset = offset + length
    return (fragment_parts[0], fragment_parts[1], fragment_parts[2].reshape(FEATURE_WIDTH, 2 * OUTER_LATENT), fragment_parts[3], fragment_parts[4].reshape(OUTER_LATENT * OUTER_LATENT, COUPLING_WIDTH), fragment_parts[5], fragment_parts[6].reshape(SYMBOL_KINDS, FEATURE_WIDTH))

def adam_update(master, moment_one, moment_two, gradient, clip_factor):
    scaled = gradient * clip_factor
    first = beta_first * moment_one + (1.0 - beta_first) * scaled
    second = beta_second * moment_two + (1.0 - beta_second) * scaled * scaled
    fix_first = 1.0 - beta_first ** STEP
    fix_second = 1.0 - beta_second ** STEP
    update = first / fix_first / (jnp.sqrt(second / fix_second) + adam_eps)
    return (master - learn_rate * update, first, second)

def per_crop_gradient(token_identifiers, crop_mask_slice, pair_crop_slice, sequence_crop_slice, layer_weights):
    gain, shift, w_pair, b_pair, w_out, b_out, table = layer_weights
    multiplier = 1.0 / HOMOLOG_DEPTH
    embedded = table[token_identifiers]
    floats = embedded.astype(jnp.float32)
    center = lax.optimization_barrier(jnp.mean(floats, axis=-1, keepdims=True))
    variance = lax.optimization_barrier(jnp.mean((floats - center) ** 2, axis=-1, keepdims=True))
    inverse_count = lax.rsqrt(variance + norm_eps)
    unit_vector = (floats - center) * inverse_count
    normed = (unit_vector * gain.astype(jnp.float32) + shift.astype(jnp.float32)).astype(jnp.bfloat16)
    masked_row_count = jnp.transpose(crop_mask_slice).astype(jnp.float32)
    proj = jnp.einsum('srd,dh->rsh', normed.astype(jnp.float32), w_pair.astype(jnp.float32)) + b_pair.astype(jnp.float32)
    acts = (proj * masked_row_count[:, :, None]).astype(jnp.bfloat16)
    left = acts[:, :, :OUTER_LATENT].astype(jnp.float32)
    right = acts[:, :, OUTER_LATENT:].astype(jnp.float32)
    w_out_f = w_out.astype(jnp.float32)

    def tile_of_sites(carry, index):
        wout_acc, right_acc = carry
        left_blk = lax.dynamic_slice_in_dim(left, index * RES_DEV, RES_DEV, 0)
        pair_blk = lax.dynamic_slice_in_dim(pair_crop_slice, index * RES_DEV, RES_DEV, 0).astype(jnp.float32)
        outer = (jnp.einsum('isc,jse->ijce', left_blk, right) * multiplier).astype(jnp.bfloat16)
        outer = outer.reshape(RES_DEV, PEPTIDE_LENGTH, OUTER_LATENT * OUTER_LATENT).astype(jnp.float32)
        wout_acc = wout_acc + jnp.einsum('ijf,ijk->fk', outer, pair_blk)
        outer_grad = jnp.einsum('ijk,fk->ijf', pair_blk, w_out_f).astype(jnp.bfloat16)
        outer_grad = outer_grad.reshape(RES_DEV, PEPTIDE_LENGTH, OUTER_LATENT, OUTER_LATENT).astype(jnp.float32)
        left_term = jnp.einsum('ijce,jse->isc', outer_grad, right) * multiplier
        right_acc = right_acc + jnp.einsum('ijce,isc->jse', outer_grad, left_blk) * multiplier
        return ((wout_acc, right_acc), left_term)
    initial_carry = (jnp.zeros((OUTER_LATENT * OUTER_LATENT, COUPLING_WIDTH), jnp.float32), jnp.zeros((PEPTIDE_LENGTH, HOMOLOG_DEPTH, OUTER_LATENT), jnp.float32))
    (output_projection_sensitivity, righthand_running), lefthand_summands = lax.scan(tile_of_sites, initial_carry, jnp.arange(N_DAP))
    lefthand_running = lefthand_summands.reshape(PEPTIDE_LENGTH, HOMOLOG_DEPTH, OUTER_LATENT)
    act_grad = (jnp.concatenate([lefthand_running, righthand_running], axis=-1) * masked_row_count[:, :, None]).astype(jnp.bfloat16)
    act_f = act_grad.astype(jnp.float32)
    wpair_grad = jnp.einsum('srd,rsh->dh', normed.astype(jnp.float32), act_f)
    bpair_grad = lax.optimization_barrier(jnp.sum(act_f, axis=(0, 1)))
    norm_grad = jnp.einsum('rsh,dh->srd', act_f, w_pair.astype(jnp.float32))
    gain_grad = lax.optimization_barrier(jnp.sum(norm_grad * unit_vector, axis=(0, 1)))
    shift_grad = lax.optimization_barrier(jnp.sum(norm_grad, axis=(0, 1)))
    clipped_gradient = norm_grad * gain.astype(jnp.float32)
    lookup_table_derivative = sequence_crop_slice.astype(jnp.float32) + inverse_count * (clipped_gradient - lax.optimization_barrier(jnp.mean(clipped_gradient, axis=-1, keepdims=True)) - unit_vector * lax.optimization_barrier(jnp.mean(clipped_gradient * unit_vector, axis=-1, keepdims=True)))
    indicator_matrix = (token_identifiers[:, :, None] == jnp.arange(SYMBOL_KINDS, dtype=jnp.int32)).astype(jnp.float32).reshape(-1, SYMBOL_KINDS)
    lookup_derivative = jnp.dot(indicator_matrix.T, lookup_table_derivative.reshape(-1, FEATURE_WIDTH), precision=lax.Precision.HIGHEST)
    bout_grad = lax.optimization_barrier(jnp.sum(pair_crop_slice.astype(jnp.float32), axis=(0, 1)))
    return jnp.concatenate([gain_grad, shift_grad, wpair_grad.reshape(-1), bpair_grad, output_projection_sensitivity.reshape(-1), bout_grad, lookup_derivative.reshape(-1)])

def reference(symbol_codes, aligned_validity, pair_update_cotangent, aligned_feature_adjoint, local_master_weights, local_first_moment, local_second_moment, remaining_master_weights, remaining_first_moment, remaining_second_moment, remaining_gradient):
    layer_weights = unpack(local_master_weights.astype(jnp.bfloat16))
    local_layer_gradient = jnp.zeros((PARAM_TOTAL,), jnp.float32)
    for crop_index in range(SAMPLE_WINDOWS):
        local_layer_gradient = local_layer_gradient + per_crop_gradient(symbol_codes[crop_index], aligned_validity[crop_index], pair_update_cotangent[crop_index], aligned_feature_adjoint[crop_index], layer_weights)
    total = jnp.sqrt(jnp.sum(local_layer_gradient * local_layer_gradient) + jnp.sum(remaining_gradient * remaining_gradient))
    clip_factor = jnp.minimum(1.0, clip_norm / (total + 1e-06))
    new_master, new_one, new_two = adam_update(local_master_weights, local_first_moment, local_second_moment, local_layer_gradient, clip_factor)
    rest_new, rest_one, rest_two = adam_update(remaining_master_weights, remaining_first_moment, remaining_second_moment, remaining_gradient, clip_factor)
    return (new_master, new_one, new_two, new_master.astype(jnp.bfloat16), rest_new, rest_one, rest_two, rest_new.astype(jnp.bfloat16))
```

```python
import jax
import jax.numpy as jnp
from jax import lax
from jax.experimental import pallas as pl
from jax.experimental.pallas import tpu as pltpu
from jax.sharding import PartitionSpec as P

FEATURE_WIDTH = 256
OUTER_LATENT = 32
SYMBOL_KINDS = 23
STEP = 10
PARAMS = 154048
ROWS = 1208
KINDS = 24
MASKED = 24.0
DEPTH = 128
RES = 16
LENGTH = 256
PLANE = 32
RINGS = 8
CROP = 16

SUM_BLOCK = 23
FEAT_BLOCK = 24
ACT_BLOCK = 26
BLOCKS = 27

beta_first = 0.9
beta_second = 0.999
adam_eps = 1e-06
learn_rate = 0.001
clip_norm = 0.1
norm_eps = 1e-05

MESH = pl.DeviceIdType.MESH
F32 = jnp.float32
BF16 = jnp.bfloat16


def iota(shape, axis):
    return lax.broadcasted_iota(jnp.int32, shape, axis)


def dot(a, b):
    return jnp.dot(a, b, preferred_element_type=F32)


def dot_nt(a, b):
    return lax.dot_general(a, b, (((1,), (1,)), ((), ())), preferred_element_type=F32)


def halves(x):
    high = x.astype(BF16)
    return high, (x - high.astype(F32)).astype(BF16)


def halves_f32(x):
    high = x.astype(BF16).astype(F32)
    return high, x - high


def kernel(
    tok_hbm,
    valid_hbm,
    pair_hbm,
    adj_hbm,
    w_hbm,
    rest_hbm,
    grad_ref,
    clip_ref,
    tok_v,
    valid_v,
    pair_v,
    adj_v,
    w_v,
    rest_v,
    codes,
    counts,
    part,
    recv,
    ring,
    total,
    outer_high,
    outer_low,
    shifted,
    wide,
    prod,
    pair_rows,
    local_sem,
    code_send,
    code_recv,
    plane_send,
    plane_recv,
    ring_send,
    ring_recv,
    all_send,
    all_recv,
):
    dp = lax.axis_index("dp")
    dap = lax.axis_index("dap")
    z = dap // 2
    x_hi = dap % 2
    slot = dp * 2 + x_hi

    def at_plane(p):
        return (p // 2, z * 2 + p % 2)

    loads = []
    for n, (src, dst) in enumerate(
        (
            (tok_hbm, tok_v),
            (valid_hbm, valid_v),
            (w_hbm, w_v),
            (adj_hbm, adj_v),
            (rest_hbm, rest_v),
            (pair_hbm, pair_v),
        )
    ):
        copy = pltpu.make_async_copy(src, dst, local_sem.at[n])
        copy.start()
        loads.append(copy)

    barrier = pltpu.get_barrier_semaphore()

    def greet_crop(t, carry):
        pl.semaphore_signal(
            barrier, inc=1, device_id=(dp, (dap + t) % CROP), device_id_type=MESH
        )
        return carry

    def greet_plane(t, carry):
        pl.semaphore_signal(
            barrier, inc=1, device_id=at_plane((slot + t) % PLANE), device_id_type=MESH
        )
        return carry

    lax.fori_loop(1, CROP, greet_crop, 0)
    lax.fori_loop(1, PLANE, greet_plane, 0)

    loads[0].wait()
    loads[1].wait()
    tok = tok_v[...].astype(F32)
    code = jnp.where(valid_v[...] != 0, tok, MASKED)
    own = jnp.transpose(code)
    codes[dap] = own.astype(BF16)
    pl.semaphore_wait(barrier, CROP - 1 + PLANE - 1)

    def code_copy(source, target):
        return pltpu.make_async_remote_copy(
            src_ref=codes.at[source],
            dst_ref=codes.at[source],
            send_sem=code_send.at[target],
            recv_sem=code_recv.at[source],
            device_id=(dp, target),
            device_id_type=MESH,
        )

    def send_codes(t, carry):
        code_copy(dap, (dap + t) % CROP).start()
        return carry

    lax.fori_loop(1, CROP, send_codes, 0)

    spread = (iota((RES, 128), 1) % RES == iota((RES, 128), 0)).astype(F32)
    tiled = dot(tok, spread)
    tiled = jnp.where(iota((DEPTH, 128), 0) % 8 == iota((DEPTH, 128), 1) // RES, tiled, 0.0)
    gather = (iota((RES, DEPTH), 1) // 8 == iota((RES, DEPTH), 0)).astype(F32)
    flat = dot(gather, tiled)
    kind = iota((KINDS, 128), 0).astype(F32)
    hot = jnp.concatenate(
        [(flat[q : q + 1, :] == kind).astype(F32) for q in range(RES)], axis=1
    ).astype(BF16)
    loads[3].wait()
    feat = dot(hot, adj_v[...])
    part[FEAT_BLOCK] = feat[:, :128]
    part[FEAT_BLOCK + 1] = feat[:, 128:]

    loads[4].wait()
    rest = rest_v[...]
    square = jnp.sum((rest * rest).reshape(32, 8, 512), axis=0)
    square = square[:, :128] + square[:, 128:256] + square[:, 256:384] + square[:, 384:]

    loads[2].wait()
    weights = w_v[...].astype(BF16).astype(F32)
    low_lane = iota((1, 128), 1) < 64
    shifted[0:ROWS] = pltpu.roll(weights, 64, 1)
    w_out = jnp.where(low_lane, shifted[pl.ds(132, 1024), :], shifted[pl.ds(133, 1024), :])
    first = jnp.where(
        low_lane,
        shifted[pl.ds(1157, KINDS, stride=2), :],
        shifted[pl.ds(1158, KINDS, stride=2), :],
    )
    second = jnp.where(
        low_lane,
        shifted[pl.ds(1158, KINDS, stride=2), :],
        shifted[pl.ds(1159, KINDS, stride=2), :],
    )
    table = jnp.concatenate([first, second], axis=1)
    table = jnp.where(iota((KINDS, FEATURE_WIDTH), 0) < SYMBOL_KINDS, table, 0.0)
    center = jnp.mean(table, axis=1, keepdims=True)
    variance = jnp.mean((table - center) ** 2, axis=1, keepdims=True)
    inverse = lax.rsqrt(variance + norm_eps)
    unit = (table - center) * inverse
    gain = jnp.concatenate([weights[0:1], weights[1:2]], axis=1)
    shift = jnp.concatenate([weights[2:3], weights[3:4]], axis=1)
    normed = (unit * gain + shift).astype(BF16).astype(F32)
    w_rows = weights[4:132]
    pair_rows[pl.ds(0, 128, stride=2), :] = jnp.where(low_lane, w_rows, 0.0)
    pair_rows[pl.ds(1, 128, stride=2), :] = jnp.where(low_lane, pltpu.roll(w_rows, 64, 1), 0.0)
    w_pair = pair_rows[...]
    bias = jnp.where(low_lane, weights[132:133], 0.0)
    acts = (dot(normed, w_pair) + bias).astype(BF16).astype(F32)
    acts = jnp.where(iota((KINDS, 128), 0) < SYMBOL_KINDS, acts, 0.0)
    he = iota((128, 1024), 1)
    left_wide = dot(acts, (iota((128, 1024), 0) == he // 32).astype(F32))
    right_wide = dot(acts, (iota((128, 1024), 0) - 32 == he % 32).astype(F32))

    local = own
    hot_own = jnp.concatenate(
        [(local[i : i + 1, :] == kind).astype(F32) for i in range(RES)], axis=0
    ).astype(BF16)

    def wait_codes(t, carry):
        code_copy((dap + t) % CROP, dap).wait_recv()
        return carry

    lax.fori_loop(1, CROP, wait_codes, 0)
    every = jnp.transpose(codes[...].reshape(LENGTH, DEPTH).astype(F32))
    for p in range(KINDS // 2):
        pieces = []
        for v in (2 * p, 2 * p + 1):
            if v < SYMBOL_KINDS:
                hot_all = (every == float(v)).astype(F32).astype(BF16)
                pieces.append(dot(hot_own, hot_all).reshape(RES, KINDS, LENGTH))
            else:
                pieces.append(jnp.ones((RES, KINDS, LENGTH), F32))
        both = jnp.concatenate(pieces, axis=1).astype(BF16)
        for i in range(RES):
            counts[p * 48 : p * 48 + 48, i * LENGTH : (i + 1) * LENGTH] = both[i]
    loads[5].wait()
    sums = dot(counts[...], pair_v[...])
    rows = iota((KINDS, 128), 0)
    part[0:SYMBOL_KINDS] = sums[: SYMBOL_KINDS * KINDS].reshape(SYMBOL_KINDS, KINDS, 128)
    last = jnp.where(rows < 8, sums[SYMBOL_KINDS * KINDS :], 0.0)
    part[SUM_BLOCK] = jnp.concatenate([last[:8], square, last[16:]], axis=0)

    def plane_copy(p, source, target):
        return pltpu.make_async_remote_copy(
            src_ref=part.at[p],
            dst_ref=recv.at[source],
            send_sem=plane_send.at[target],
            recv_sem=plane_recv.at[source],
            device_id=at_plane(target),
            device_id_type=MESH,
        )

    def send_plane(t, carry):
        p = (slot + t) % PLANE

        @pl.when(p < ACT_BLOCK)
        def _():
            plane_copy(p, slot, p).start()

        return carry

    lax.fori_loop(1, PLANE, send_plane, 0)

    high, low = halves(sums[: SYMBOL_KINDS * KINDS])
    w_out = w_out.astype(BF16)
    prod[...] = dot_nt(high, w_out) + dot_nt(low, w_out)
    left_sum = jnp.zeros((KINDS, 1024), F32)
    right_rows = []
    for v in range(SYMBOL_KINDS):
        block = prod[v * KINDS : (v + 1) * KINDS]
        left_sum = left_sum + right_wide[v : v + 1] * block
        right_rows.append(jnp.sum(left_wide * block, axis=0, keepdims=True))
    right_rows.append(jnp.zeros((1, 1024), F32))
    right_sum = jnp.concatenate(right_rows, axis=0)
    he_row = iota((1024, 128), 0)
    lane = iota((1024, 128), 1)
    fold_left = (he_row // 32 == lane).astype(F32)
    fold_right = (he_row % 32 == lane - 32).astype(F32)
    left_high, left_low = halves_f32(left_sum)
    right_high, right_low = halves_f32(right_sum)
    part[ACT_BLOCK] = (
        dot(left_high, fold_left)
        + dot(left_low, fold_left)
        + dot(right_high, fold_right)
        + dot(right_low, fold_right)
    )

    @pl.when(slot != ACT_BLOCK)
    def _():
        plane_copy(ACT_BLOCK, slot, ACT_BLOCK).start()

    tile_u = jnp.concatenate([acts] * KINDS, axis=0)
    tile_v = jnp.concatenate(
        [jnp.broadcast_to(acts[v : v + 1], (KINDS, 128)) for v in range(KINDS)], axis=0
    )
    outer = dot_nt(fold_left, tile_u) * dot_nt(fold_right, tile_v)
    outer_hi, outer_lo = halves(outer)
    outer_high[...] = outer_hi
    outer_low[...] = outer_lo

    def ring_copy(source, target):
        return pltpu.make_async_remote_copy(
            src_ref=ring.at[source],
            dst_ref=ring.at[source],
            send_sem=ring_send.at[target],
            recv_sem=ring_recv.at[source],
            device_id=(dp, target * 2 + x_hi),
            device_id_type=MESH,
        )

    def all_copy(source, target):
        return pltpu.make_async_remote_copy(
            src_ref=total.at[source],
            dst_ref=total.at[source],
            send_sem=all_send.at[target],
            recv_sem=all_recv.at[source],
            device_id=at_plane(target),
            device_id_type=MESH,
        )

    @pl.when(slot < BLOCKS)
    def _():
        recv[slot] = part[slot]

        def wait_plane(t, carry):
            p = (slot + t) % PLANE
            plane_copy(slot, p, slot).wait_recv()
            return carry

        lax.fori_loop(1, PLANE, wait_plane, 0)
        ring[z] = jnp.sum(recv[...], axis=0)

        def send_ring(t, carry):
            ring_copy(z, (z + t) % RINGS).start()
            return carry

        lax.fori_loop(1, RINGS, send_ring, 0)

        def wait_ring(t, carry):
            ring_copy((z + t) % RINGS, z).wait_recv()
            return carry

        lax.fori_loop(1, RINGS, wait_ring, 0)
        total[slot] = jnp.sum(ring[...], axis=0)

        def send_all(t, carry):
            all_copy(slot, (slot + t) % PLANE).start()
            return carry

        lax.fori_loop(1, PLANE, send_all, 0)

    def wait_all(t, carry):
        p = (slot + t) % PLANE

        @pl.when(p < BLOCKS)
        def _():
            all_copy(p, slot).wait_recv()

        return carry

    lax.fori_loop(1, PLANE, wait_all, 0)

    scale = 1.0 / DEPTH
    summed = jnp.concatenate(
        [
            total[0:SYMBOL_KINDS].reshape(SYMBOL_KINDS * KINDS, 128) * scale,
            jnp.zeros((KINDS, 128), F32),
        ],
        axis=0,
    )
    high, low = halves(summed)
    outer_hi = outer_high[...]
    w_out_grad = dot(outer_hi, high) + dot(outer_hi, low) + dot(outer_low[...], high)
    act = total[ACT_BLOCK] * scale
    act_high, act_low = halves_f32(act)
    norm_grad = dot_nt(act_high, w_pair) + dot_nt(act_low, w_pair)
    normed_t = jnp.transpose(normed)
    wide[...] = dot(normed_t, act_high) + dot(normed_t, act_low)
    w_pair_grad = wide[pl.ds(0, 128, stride=2), :] + pltpu.roll(
        wide[pl.ds(1, 128, stride=2), :], 64, 1
    )
    gained = norm_grad * gain
    feat = jnp.concatenate([total[FEAT_BLOCK], total[FEAT_BLOCK + 1]], axis=1)
    table_grad = feat + inverse * (
        gained
        - jnp.mean(gained, axis=1, keepdims=True)
        - unit * jnp.mean(gained * unit, axis=1, keepdims=True)
    )
    gain_grad = jnp.sum(norm_grad * unit, axis=0, keepdims=True)
    shift_grad = jnp.sum(norm_grad, axis=0, keepdims=True)
    bias_grad = jnp.sum(act, axis=0, keepdims=True)

    shifted[0:8] = jnp.zeros((8, 128), F32)
    shifted[8:1032] = pltpu.roll(w_out_grad, 64, 1)
    shifted[1032:1088] = jnp.zeros((56, 128), F32)
    shifted[1032:1033] = pltpu.roll(total[SUM_BLOCK][0:1], 64, 1)
    shifted[pl.ds(1033, SYMBOL_KINDS, stride=2), :] = pltpu.roll(
        table_grad[:SYMBOL_KINDS, :128], 64, 1
    )
    shifted[pl.ds(1034, SYMBOL_KINDS, stride=2), :] = pltpu.roll(
        table_grad[:SYMBOL_KINDS, 128:], 64, 1
    )
    grad_ref[128:ROWS] = jnp.where(low_lane, shifted[3:1083], shifted[4:1084])
    grad_ref[0:4] = jnp.concatenate(
        [gain_grad[:, :128], gain_grad[:, 128:], shift_grad[:, :128], shift_grad[:, 128:]], axis=0
    )
    grad_ref[4:132] = w_pair_grad
    grad_ref[132:133] = jnp.where(low_lane, bias_grad, grad_ref[132:133])
    grad = grad_ref[...]
    norm = jnp.sum(jnp.sum((grad * grad).reshape(ROWS // 8, 8, 128), axis=0) + total[SUM_BLOCK][8:16])
    norm = jnp.sqrt(jnp.full((1, 512), norm, F32))
    clip_ref[...] = jnp.minimum(1.0, clip_norm / (norm + 1e-06))

    def finish_codes(t, carry):
        code_copy(dap, (dap + t) % CROP).wait_send()
        return carry

    lax.fori_loop(1, CROP, finish_codes, 0)

    def finish_plane(t, carry):
        p = (slot + t) % PLANE

        @pl.when(p < BLOCKS)
        def _():
            plane_copy(p, slot, p).wait_send()

        return carry

    lax.fori_loop(1, PLANE, finish_plane, 0)

    @pl.when(slot < BLOCKS)
    def _():
        def finish_ring(t, carry):
            ring_copy(z, (z + t) % RINGS).wait_send()
            return carry

        lax.fori_loop(1, RINGS, finish_ring, 0)

        def finish_all(t, carry):
            all_copy(slot, (slot + t) % PLANE).wait_send()
            return carry

        lax.fori_loop(1, PLANE, finish_all, 0)


def gradients(tok, valid, pair, adj, weights, rest):
    anywhere = pl.BlockSpec(memory_space=pl.ANY)
    return pl.pallas_call(
        kernel,
        out_shape=(
            jax.ShapeDtypeStruct((ROWS, 128), F32),
            jax.ShapeDtypeStruct((1, 512), F32),
        ),
        in_specs=[anywhere] * 6,
        out_specs=(
            pl.BlockSpec(memory_space=pltpu.VMEM),
            pl.BlockSpec(memory_space=pltpu.VMEM),
        ),
        scratch_shapes=[
            pltpu.VMEM((DEPTH, RES), jnp.int32),
            pltpu.VMEM((DEPTH, RES), jnp.int32),
            pltpu.VMEM((RES * LENGTH, 128), BF16),
            pltpu.VMEM((DEPTH * RES, FEATURE_WIDTH), BF16),
            pltpu.VMEM((ROWS, 128), F32),
            pltpu.VMEM((256, 512), F32),
            pltpu.VMEM((CROP, RES, DEPTH), BF16),
            pltpu.VMEM((KINDS * KINDS, RES * LENGTH), BF16),
            pltpu.VMEM((BLOCKS, KINDS, 128), F32),
            pltpu.VMEM((PLANE, KINDS, 128), F32),
            pltpu.VMEM((RINGS, KINDS, 128), F32),
            pltpu.VMEM((BLOCKS, KINDS, 128), F32),
            pltpu.VMEM((1024, KINDS * KINDS), BF16),
            pltpu.VMEM((1024, KINDS * KINDS), BF16),
            pltpu.VMEM((ROWS + 8, 128), F32),
            pltpu.VMEM((FEATURE_WIDTH, 128), F32),
            pltpu.VMEM((SYMBOL_KINDS * KINDS, 1024), F32),
            pltpu.VMEM((FEATURE_WIDTH, 128), F32),
            pltpu.SemaphoreType.DMA((6,)),
            pltpu.SemaphoreType.DMA((CROP,)),
            pltpu.SemaphoreType.DMA((CROP,)),
            pltpu.SemaphoreType.DMA((PLANE,)),
            pltpu.SemaphoreType.DMA((PLANE,)),
            pltpu.SemaphoreType.DMA((RINGS,)),
            pltpu.SemaphoreType.DMA((RINGS,)),
            pltpu.SemaphoreType.DMA((PLANE,)),
            pltpu.SemaphoreType.DMA((PLANE,)),
        ],
        compiler_params=pltpu.CompilerParams(
            collective_id=0, has_side_effects=True, vmem_limit_bytes=40 * 1024 * 1024
        ),
        cost_estimate=pl.CostEstimate(
            flops=3_000_000_000, bytes_accessed=4_000_000, transcendentals=0
        ),
    )(tok, valid, pair, adj, weights, rest)


def adam_update(master, moment_one, moment_two, gradient, clip_factor):
    scaled = gradient * clip_factor
    first = beta_first * moment_one + (1.0 - beta_first) * scaled
    second = beta_second * moment_two + (1.0 - beta_second) * scaled * scaled
    fix_first = 1.0 - beta_first**STEP
    fix_second = 1.0 - beta_second**STEP
    update = first / fix_first / (jnp.sqrt(second / fix_second) + adam_eps)
    return (master - learn_rate * update, first, second)


def shards(
    symbol_codes,
    aligned_validity,
    pair_update_cotangent,
    aligned_feature_adjoint,
    local_master_weights,
    local_first_moment,
    local_second_moment,
    remaining_master_weights,
    remaining_first_moment,
    remaining_second_moment,
    remaining_gradient,
):
    weights = jnp.pad(local_master_weights, (0, ROWS * 128 - PARAMS)).reshape(ROWS, 128)
    gradient, clip = gradients(
        symbol_codes[0],
        aligned_validity[0],
        pair_update_cotangent.reshape(RES * LENGTH, 128),
        aligned_feature_adjoint.reshape(DEPTH * RES, FEATURE_WIDTH),
        weights,
        remaining_gradient,
    )
    local_layer_gradient = gradient.reshape(-1)[:PARAMS]
    new_master, new_one, new_two = adam_update(
        local_master_weights,
        local_first_moment,
        local_second_moment,
        local_layer_gradient,
        clip[0, 0],
    )
    rest_new, rest_one, rest_two = adam_update(
        remaining_master_weights,
        remaining_first_moment,
        remaining_second_moment,
        remaining_gradient,
        clip,
    )
    return (
        new_master,
        new_one,
        new_two,
        new_master.astype(BF16),
        rest_new,
        rest_one,
        rest_two,
        rest_new.astype(BF16),
    )


def solution(mesh):
    return jax.shard_map(
        shards,
        mesh=mesh,
        in_specs=(
            P("dp", None, "dap"),
            P("dp", None, "dap"),
            P("dp", "dap", None, None),
            P("dp", None, "dap", None),
            P(),
            P(),
            P(),
            P(("dp", "dap"), None),
            P(("dp", "dap"), None),
            P(("dp", "dap"), None),
            P(("dp", "dap"), None),
        ),
        out_specs=(
            P(),
            P(),
            P(),
            P(),
            P(("dp", "dap"), None),
            P(("dp", "dap"), None),
            P(("dp", "dap"), None),
            P(("dp", "dap"), None),
        ),
        check_vma=False,
    )
```

```python
import jax
import jax.numpy as jnp
from jax import lax
from jax.experimental import pallas as pl
from jax.experimental.pallas import tpu as pltpu
from jax.sharding import PartitionSpec as P

FEATURE_WIDTH = 256
OUTER_LATENT = 32
SYMBOL_KINDS = 23
STEP = 10
PARAMS = 154048
ROWS = 1208
KINDS = 24
MASKED = 24.0
DEPTH = 128
RES = 16
LENGTH = 256
PLANE = 32
RINGS = 8

PAIR_ROWS = 32
PAIR_BLOCKS = 18
FEAT_BLOCK = 0
SUM_BLOCK = 2
ACT_BLOCK = 3
BLOCKS = PAIR_BLOCKS + 4
CHUNKS = 4

beta_first = 0.9
beta_second = 0.999
adam_eps = 1e-06
learn_rate = 0.001
clip_norm = 0.1
norm_eps = 1e-05

MESH = pl.DeviceIdType.MESH
F32 = jnp.float32
BF16 = jnp.bfloat16


def ring_hops(step, size):
    return min(step, size - step)


PLANE_STEPS = sorted(
    ((dx, dy, dc) for dx in range(4) for dy in range(4) for dc in range(2) if dx + dy + dc > 0),
    key=lambda s: -ring_hops(s[0], 4) - ring_hops(s[1], 4),
)
RING_STEPS = sorted(range(1, RINGS), key=lambda s: -ring_hops(s, RINGS))


def iota(shape, axis):
    return lax.broadcasted_iota(jnp.int32, shape, axis)


def dot(a, b):
    return jnp.dot(a, b, preferred_element_type=F32)


def dot_nt(a, b):
    return lax.dot_general(a, b, (((1,), (1,)), ((), ())), preferred_element_type=F32)


def dot_tn(a, b):
    return lax.dot_general(a, b, (((0,), (0,)), ((), ())), preferred_element_type=F32)


def halves(x):
    high = x.astype(BF16)
    return high, (x - high.astype(F32)).astype(BF16)


def halves_f32(x):
    high = x.astype(BF16).astype(F32)
    return high, x - high


def kernel(
    tok_hbm,
    valid_hbm,
    pair_hbm,
    adj_hbm,
    w_hbm,
    rest_hbm,
    grad_ref,
    clip_ref,
    tok_v,
    valid_v,
    pair_v,
    adj_v,
    w_v,
    rest_v,
    codes,
    counts,
    pair_part,
    pair_recv,
    pair_ring,
    pair_total,
    wide_part,
    wide_recv,
    wide_ring,
    wide_total,
    outer_high,
    outer_low,
    shifted,
    wide,
    prod,
    pair_rows,
    local_sem,
    code_send,
    code_recv,
    half_send,
    half_recv,
    plane_send,
    plane_recv,
    ring_send,
    ring_recv,
    all_send,
    all_recv,
):
    dp = lax.axis_index("dp")
    dap = lax.axis_index("dap")
    z = dap // 2
    x_hi = dap % 2
    core = dp % 2
    y = (dp // 2) % 4
    x = x_hi * 2 + dp // 8

    def place(x, y, core):
        return core * 16 + (x % 2) * 8 + y * 2 + x // 2

    def at_plane(p):
        return ((p % 16 // 2) * 2 + p // 16, z * 2 + p % 2)

    slot = place(x, y, core)
    peers = [
        place((x + dx) % 4, (y + dy) % 4, (core + dc) % 2) for dx, dy, dc in PLANE_STEPS
    ]

    loads = []
    for n, (src, dst) in enumerate(
        (
            (tok_hbm, tok_v),
            (valid_hbm, valid_v),
            (w_hbm, w_v),
            (adj_hbm, adj_v),
            (rest_hbm, rest_v),
            (pair_hbm, pair_v),
        )
    ):
        copy = pltpu.make_async_copy(src, dst, local_sem.at[n])
        copy.start()
        loads.append(copy)

    barrier = pltpu.get_barrier_semaphore()
    for step in RING_STEPS:
        pl.semaphore_signal(
            barrier,
            inc=1,
            device_id=(dp, (z + step) % RINGS * 2 + x_hi),
            device_id_type=MESH,
        )
    for p in peers:
        pl.semaphore_signal(barrier, inc=1, device_id=at_plane(p), device_id_type=MESH)

    loads[0].wait()
    loads[1].wait()
    tok = tok_v[...].astype(F32)
    own = jnp.where(valid_v[...] != 0, tok, MASKED)
    codes[x_hi, z] = own.astype(BF16)
    pl.semaphore_wait(barrier, RINGS - 1 + PLANE - 1)

    def code_copy(source, target):
        return pltpu.make_async_remote_copy(
            src_ref=codes.at[x_hi, source],
            dst_ref=codes.at[x_hi, source],
            send_sem=code_send.at[target],
            recv_sem=code_recv.at[source],
            device_id=(dp, target * 2 + x_hi),
            device_id_type=MESH,
        )

    def half_copy(half):
        return pltpu.make_async_remote_copy(
            src_ref=codes.at[half],
            dst_ref=codes.at[half],
            send_sem=half_send,
            recv_sem=half_recv,
            device_id=(dp, z * 2 + 1 - x_hi),
            device_id_type=MESH,
        )

    for step in RING_STEPS:
        code_copy(z, (z + step) % RINGS).start()

    spread = (iota((RES, 128), 1) % RES == iota((RES, 128), 0)).astype(F32)
    tiled = dot_tn(tok, spread)
    tiled = jnp.where(iota((DEPTH, 128), 0) % 8 == iota((DEPTH, 128), 1) // RES, tiled, 0.0)
    gather = (iota((RES, DEPTH), 1) // 8 == iota((RES, DEPTH), 0)).astype(F32)
    flat = dot(gather, tiled)
    kind = iota((KINDS, 128), 0).astype(F32)
    hot = jnp.concatenate(
        [(flat[q : q + 1, :] == kind).astype(F32) for q in range(RES)], axis=1
    ).astype(BF16)
    loads[3].wait()
    feat = dot(hot, adj_v[...])
    wide_part[FEAT_BLOCK] = feat[:, :128]
    wide_part[FEAT_BLOCK + 1] = feat[:, 128:]

    loads[4].wait()
    rest = rest_v[...]
    square = jnp.sum((rest * rest).reshape(32, 8, 512), axis=0)
    square = square[:, :128] + square[:, 128:256] + square[:, 256:384] + square[:, 384:]

    loads[2].wait()
    weights = jnp.concatenate(
        [
            w_v[pl.ds(0, 153600)].reshape(1200, 128),
            jnp.concatenate(
                [w_v[pl.ds(153600, PARAMS - 153600)], jnp.zeros((ROWS * 128 - PARAMS,), F32)]
            ).reshape(8, 128),
        ],
        axis=0,
    )
    weights = weights.astype(BF16).astype(F32)
    low_lane = iota((1, 128), 1) < 64
    shifted[0:ROWS] = pltpu.roll(weights, 64, 1)
    w_out = jnp.where(low_lane, shifted[pl.ds(132, 1024), :], shifted[pl.ds(133, 1024), :])
    first = jnp.where(
        low_lane,
        shifted[pl.ds(1157, KINDS, stride=2), :],
        shifted[pl.ds(1158, KINDS, stride=2), :],
    )
    second = jnp.where(
        low_lane,
        shifted[pl.ds(1158, KINDS, stride=2), :],
        shifted[pl.ds(1159, KINDS, stride=2), :],
    )
    table = jnp.concatenate([first, second], axis=1)
    table = jnp.where(iota((KINDS, FEATURE_WIDTH), 0) < SYMBOL_KINDS, table, 0.0)
    center = jnp.mean(table, axis=1, keepdims=True)
    variance = jnp.mean((table - center) ** 2, axis=1, keepdims=True)
    inverse = lax.rsqrt(variance + norm_eps)
    unit = (table - center) * inverse
    gain = jnp.concatenate([weights[0:1], weights[1:2]], axis=1)
    shift = jnp.concatenate([weights[2:3], weights[3:4]], axis=1)
    normed = (unit * gain + shift).astype(BF16).astype(F32)
    w_rows = weights[4:132]
    pair_rows[pl.ds(0, 128, stride=2), :] = jnp.where(low_lane, w_rows, 0.0)
    pair_rows[pl.ds(1, 128, stride=2), :] = jnp.where(low_lane, pltpu.roll(w_rows, 64, 1), 0.0)
    w_pair = pair_rows[...]
    bias = jnp.where(low_lane, weights[132:133], 0.0)
    acts = (dot(normed, w_pair) + bias).astype(BF16).astype(F32)
    acts = jnp.where(iota((KINDS, 128), 0) < SYMBOL_KINDS, acts, 0.0)
    he = iota((128, 1024), 1)
    left_wide = dot(acts, (iota((128, 1024), 0) == he // 32).astype(F32))
    right_wide = dot(acts, (iota((128, 1024), 0) - 32 == he % 32).astype(F32))

    hot_own = jnp.concatenate(
        [(own[i : i + 1, :] == kind).astype(F32) for i in range(RES)], axis=0
    ).astype(BF16)

    for step in RING_STEPS:
        code_copy((z + step) % RINGS, z).wait_recv()
    half_copy(x_hi).start()
    half_copy(1 - x_hi).wait_recv()
    every = jnp.transpose(codes[...].astype(F32), (1, 0, 2, 3)).reshape(LENGTH, DEPTH)
    every = jnp.transpose(every)
    for p in range(KINDS // 2):
        pieces = []
        for v in (2 * p, 2 * p + 1):
            if v < SYMBOL_KINDS:
                hot_all = (every == float(v)).astype(F32).astype(BF16)
                pieces.append(dot(hot_own, hot_all).reshape(RES, KINDS, LENGTH))
            else:
                pieces.append(jnp.ones((RES, KINDS, LENGTH), F32))
        both = jnp.concatenate(pieces, axis=1).astype(BF16)
        for i in range(RES):
            counts[p * 48 : p * 48 + 48, i * LENGTH : (i + 1) * LENGTH] = both[i]
    loads[5].wait()
    sums = dot(counts[...], pair_v[...])
    pair_part[...] = sums.astype(BF16).reshape(PAIR_BLOCKS, PAIR_ROWS, 128)
    rows = iota((KINDS, 128), 0)
    last = jnp.where(rows < 8, sums[SYMBOL_KINDS * KINDS :], 0.0)
    wide_part[SUM_BLOCK] = jnp.concatenate([last[:8], square, last[16:]], axis=0)

    def plane_copy(part, recv, block, source, target):
        return pltpu.make_async_remote_copy(
            src_ref=part.at[block],
            dst_ref=recv.at[source],
            send_sem=plane_send.at[target],
            recv_sem=plane_recv.at[source],
            device_id=at_plane(target),
            device_id_type=MESH,
        )

    def pair_copy(block, source, target):
        return plane_copy(pair_part, pair_recv, block, source, target)

    def wide_copy(block, source, target):
        return plane_copy(wide_part, wide_recv, block, source, target)

    for p in peers:

        @pl.when(p < PAIR_BLOCKS)
        def _():
            pair_copy(p, slot, p).start()

        @pl.when((p >= PAIR_BLOCKS) & (p < PAIR_BLOCKS + ACT_BLOCK))
        def _():
            wide_copy(p - PAIR_BLOCKS, slot, p).start()

    high, low = halves(sums[: SYMBOL_KINDS * KINDS])
    w_out = w_out.astype(BF16)
    prod[...] = dot_nt(high, w_out) + dot_nt(low, w_out)
    left_sum = jnp.zeros((KINDS, 1024), F32)
    right_rows = []
    for v in range(SYMBOL_KINDS):
        block = prod[v * KINDS : (v + 1) * KINDS]
        left_sum = left_sum + right_wide[v : v + 1] * block
        right_rows.append(jnp.sum(left_wide * block, axis=0, keepdims=True))
    right_rows.append(jnp.zeros((1, 1024), F32))
    right_sum = jnp.concatenate(right_rows, axis=0)
    he_row = iota((1024, 128), 0)
    lane = iota((1024, 128), 1)
    fold_left = (he_row // 32 == lane).astype(F32)
    fold_right = (he_row % 32 == lane - 32).astype(F32)
    left_high, left_low = halves_f32(left_sum)
    right_high, right_low = halves_f32(right_sum)
    wide_part[ACT_BLOCK] = (
        dot(left_high, fold_left)
        + dot(left_low, fold_left)
        + dot(right_high, fold_right)
        + dot(right_low, fold_right)
    )

    @pl.when(slot != PAIR_BLOCKS + ACT_BLOCK)
    def _():
        wide_copy(ACT_BLOCK, slot, PAIR_BLOCKS + ACT_BLOCK).start()

    tile_u = jnp.concatenate([acts] * KINDS, axis=0)
    tile_v = jnp.concatenate(
        [jnp.broadcast_to(acts[v : v + 1], (KINDS, 128)) for v in range(KINDS)], axis=0
    )
    outer = dot_nt(fold_left, tile_u) * dot_nt(fold_right, tile_v) * (1.0 / DEPTH)
    outer_hi, outer_lo = halves(outer)
    outer_high[...] = outer_hi
    outer_low[...] = outer_lo

    def ring_copy(ring, source, target):
        return pltpu.make_async_remote_copy(
            src_ref=ring.at[source],
            dst_ref=ring.at[source],
            send_sem=ring_send.at[target],
            recv_sem=ring_recv.at[source],
            device_id=(dp, target * 2 + x_hi),
            device_id_type=MESH,
        )

    def all_copy(total, block, source, target):
        return pltpu.make_async_remote_copy(
            src_ref=total.at[block],
            dst_ref=total.at[block],
            send_sem=all_send.at[target],
            recv_sem=all_recv.at[source],
            device_id=at_plane(target),
            device_id_type=MESH,
        )

    def reduce(block, part, recv, ring, total):
        recv[slot] = part[block]
        for p in peers:
            plane_copy(part, recv, block, p, slot).wait_recv()
        ring[z] = jnp.sum(recv[...].astype(F32), axis=0).astype(ring.dtype)
        for step in RING_STEPS:
            ring_copy(ring, z, (z + step) % RINGS).start()
        for step in RING_STEPS:
            ring_copy(ring, (z + step) % RINGS, z).wait_recv()
        total[block] = jnp.sum(ring[...].astype(F32), axis=0).astype(total.dtype)
        for p in peers:
            all_copy(total, block, slot, p).start()

    @pl.when(slot < PAIR_BLOCKS)
    def _():
        reduce(slot, pair_part, pair_recv, pair_ring, pair_total)

    @pl.when((slot >= PAIR_BLOCKS) & (slot < BLOCKS))
    def _():
        reduce(slot - PAIR_BLOCKS, wide_part, wide_recv, wide_ring, wide_total)

    for p in peers:

        @pl.when(p < PAIR_BLOCKS)
        def _():
            all_copy(pair_total, p, p, slot).wait_recv()

        @pl.when((p >= PAIR_BLOCKS) & (p < BLOCKS))
        def _():
            all_copy(wide_total, p - PAIR_BLOCKS, p, slot).wait_recv()

    summed = pair_total[...].reshape(KINDS * KINDS, 128)
    w_out_grad = dot(outer_high[...], summed) + dot(outer_low[...], summed)
    act = wide_total[ACT_BLOCK] * (1.0 / DEPTH)
    act_high, act_low = halves_f32(act)
    norm_grad = dot_nt(act_high, w_pair) + dot_nt(act_low, w_pair)
    normed_t = jnp.transpose(normed)
    wide[...] = dot(normed_t, act_high) + dot(normed_t, act_low)
    w_pair_grad = wide[pl.ds(0, 128, stride=2), :] + pltpu.roll(
        wide[pl.ds(1, 128, stride=2), :], 64, 1
    )
    gained = norm_grad * gain
    feat = jnp.concatenate([wide_total[FEAT_BLOCK], wide_total[FEAT_BLOCK + 1]], axis=1)
    table_grad = feat + inverse * (
        gained
        - jnp.mean(gained, axis=1, keepdims=True)
        - unit * jnp.mean(gained * unit, axis=1, keepdims=True)
    )
    gain_grad = jnp.sum(norm_grad * unit, axis=0, keepdims=True)
    shift_grad = jnp.sum(norm_grad, axis=0, keepdims=True)
    bias_grad = jnp.sum(act, axis=0, keepdims=True)

    shifted[0:8] = jnp.zeros((8, 128), F32)
    shifted[8:1032] = pltpu.roll(w_out_grad, 64, 1)
    shifted[1032:1088] = jnp.zeros((56, 128), F32)
    shifted[1032:1033] = pltpu.roll(wide_total[SUM_BLOCK][0:1], 64, 1)
    shifted[pl.ds(1033, SYMBOL_KINDS, stride=2), :] = pltpu.roll(
        table_grad[:SYMBOL_KINDS, :128], 64, 1
    )
    shifted[pl.ds(1034, SYMBOL_KINDS, stride=2), :] = pltpu.roll(
        table_grad[:SYMBOL_KINDS, 128:], 64, 1
    )
    grad_ref[128:ROWS] = jnp.where(low_lane, shifted[3:1083], shifted[4:1084])
    grad_ref[0:4] = jnp.concatenate(
        [gain_grad[:, :128], gain_grad[:, 128:], shift_grad[:, :128], shift_grad[:, 128:]], axis=0
    )
    grad_ref[4:132] = w_pair_grad
    grad_ref[132:133] = jnp.where(low_lane, bias_grad, grad_ref[132:133])
    grad = grad_ref[...]
    squares = jnp.sum((grad * grad).reshape(ROWS // 8, 8, 128), axis=0)
    norm = jnp.sum(squares + wide_total[SUM_BLOCK][8:16])
    norm = jnp.sqrt(jnp.full((1, 512), norm, F32))
    clip_ref[...] = jnp.minimum(1.0, clip_norm / (norm + 1e-06))

    for step in RING_STEPS:
        code_copy(z, (z + step) % RINGS).wait_send()
    half_copy(x_hi).wait_send()
    for p in peers:

        @pl.when(p < PAIR_BLOCKS)
        def _():
            pair_copy(p, slot, p).wait_send()

        @pl.when((p >= PAIR_BLOCKS) & (p < BLOCKS))
        def _():
            wide_copy(p - PAIR_BLOCKS, slot, p).wait_send()

    def finish(block, ring, total):
        for step in RING_STEPS:
            ring_copy(ring, z, (z + step) % RINGS).wait_send()
        for p in peers:
            all_copy(total, block, slot, p).wait_send()

    @pl.when(slot < PAIR_BLOCKS)
    def _():
        finish(slot, pair_ring, pair_total)

    @pl.when((slot >= PAIR_BLOCKS) & (slot < BLOCKS))
    def _():
        finish(slot - PAIR_BLOCKS, wide_ring, wide_total)


def in_hbm(array):
    return pltpu.with_memory_space_constraint(array, pltpu.HBM)


def gradients(*arrays):
    return pl.pallas_call(
        kernel,
        out_shape=(
            jax.ShapeDtypeStruct((ROWS, 128), F32),
            jax.ShapeDtypeStruct((1, 512), F32),
        ),
        in_specs=[pl.BlockSpec(memory_space=pltpu.HBM)] * 6,
        out_specs=(
            pl.BlockSpec(memory_space=pltpu.VMEM),
            pl.BlockSpec(memory_space=pltpu.VMEM),
        ),
        scratch_shapes=[
            pltpu.VMEM((RES, DEPTH), jnp.int32),
            pltpu.VMEM((RES, DEPTH), jnp.int32),
            pltpu.VMEM((RES * LENGTH, 128), BF16),
            pltpu.VMEM((DEPTH * RES, FEATURE_WIDTH), BF16),
            pltpu.VMEM((PARAMS,), F32),
            pltpu.VMEM((256, 512), F32),
            pltpu.VMEM((2, RINGS, RES, DEPTH), BF16),
            pltpu.VMEM((KINDS * KINDS, RES * LENGTH), BF16),
            pltpu.VMEM((PAIR_BLOCKS, PAIR_ROWS, 128), BF16),
            pltpu.VMEM((PLANE, PAIR_ROWS, 128), BF16),
            pltpu.VMEM((RINGS, PAIR_ROWS, 128), BF16),
            pltpu.VMEM((PAIR_BLOCKS, PAIR_ROWS, 128), BF16),
            pltpu.VMEM((4, KINDS, 128), F32),
            pltpu.VMEM((PLANE, KINDS, 128), F32),
            pltpu.VMEM((RINGS, KINDS, 128), F32),
            pltpu.VMEM((4, KINDS, 128), F32),
            pltpu.VMEM((1024, KINDS * KINDS), BF16),
            pltpu.VMEM((1024, KINDS * KINDS), BF16),
            pltpu.VMEM((ROWS + 8, 128), F32),
            pltpu.VMEM((FEATURE_WIDTH, 128), F32),
            pltpu.VMEM((SYMBOL_KINDS * KINDS, 1024), F32),
            pltpu.VMEM((FEATURE_WIDTH, 128), F32),
            pltpu.SemaphoreType.DMA((6,)),
            pltpu.SemaphoreType.DMA((RINGS,)),
            pltpu.SemaphoreType.DMA((RINGS,)),
            pltpu.SemaphoreType.DMA,
            pltpu.SemaphoreType.DMA,
            pltpu.SemaphoreType.DMA((PLANE,)),
            pltpu.SemaphoreType.DMA((PLANE,)),
            pltpu.SemaphoreType.DMA((RINGS,)),
            pltpu.SemaphoreType.DMA((RINGS,)),
            pltpu.SemaphoreType.DMA((PLANE,)),
            pltpu.SemaphoreType.DMA((PLANE,)),
        ],
        compiler_params=pltpu.CompilerParams(
            collective_id=0, has_side_effects=True, vmem_limit_bytes=40 * 1024 * 1024
        ),
        cost_estimate=pl.CostEstimate(
            flops=3_000_000_000, bytes_accessed=40_000_000, transcendentals=0
        ),
    )(*[in_hbm(array) for array in arrays])


def adam_update(master, moment_one, moment_two, scaled):
    first = beta_first * moment_one + (1.0 - beta_first) * scaled
    second = beta_second * moment_two + (1.0 - beta_second) * scaled * scaled
    fix_first = 1.0 - beta_first**STEP
    fix_second = 1.0 - beta_second**STEP
    update = first * (learn_rate / fix_first) / (jnp.sqrt(second * (1.0 / fix_second)) + adam_eps)
    return (master - update, first, second)


def update_kernel(
    grad_ref,
    clip_ref,
    master_ref,
    one_ref,
    two_ref,
    rest_grad_ref,
    rest_master_ref,
    rest_one_ref,
    rest_two_ref,
    *refs,
):
    outs, held, sems = refs[:8], refs[8:16], refs[16]
    clip = clip_ref[...]
    rest_step = rest_grad_ref.shape[0] // CHUNKS
    flat_step = 1024 * 38
    copies = []

    def send(n, where):
        copy = pltpu.make_async_copy(held[n].at[where], outs[n].at[where], sems.at[len(copies)])
        copy.start()
        copies.append(copy)

    for chunk in range(CHUNKS):
        where = pl.ds(chunk * rest_step, rest_step)
        new = adam_update(
            rest_master_ref[where], rest_one_ref[where], rest_two_ref[where], rest_grad_ref[where] * clip
        )
        for n, value in enumerate(new + (new[0],)):
            held[4 + n][where] = value.astype(held[4 + n].dtype)
            send(4 + n, where)
    factor = jnp.max(clip)
    for chunk in range(CHUNKS):
        start = chunk * flat_step
        where = pl.ds(start, min(flat_step, PARAMS - start))
        new = adam_update(master_ref[where], one_ref[where], two_ref[where], grad_ref[where] * factor)
        for n, value in enumerate(new + (new[0],)):
            held[n][where] = value.astype(held[n].dtype)
            send(n, where)
    for copy in copies:
        copy.wait()


def updates(grad, clip, master, one, two, rest_grad, rest_master, rest_one, rest_two):
    flat = [jax.ShapeDtypeStruct(master.shape, dtype) for dtype in (F32, F32, F32, BF16)]
    rows = [jax.ShapeDtypeStruct(rest_master.shape, dtype) for dtype in (F32, F32, F32, BF16)]
    return pl.pallas_call(
        update_kernel,
        out_shape=tuple(flat + rows),
        in_specs=[pl.BlockSpec(memory_space=pltpu.VMEM)] * 9,
        out_specs=tuple([pl.BlockSpec(memory_space=pltpu.HBM)] * 8),
        scratch_shapes=[pltpu.VMEM(out.shape, out.dtype) for out in flat + rows]
        + [pltpu.SemaphoreType.DMA((8 * CHUNKS,))],
        compiler_params=pltpu.CompilerParams(vmem_limit_bytes=20 * 1024 * 1024),
        cost_estimate=pl.CostEstimate(
            flops=5_000_000, bytes_accessed=8_000_000, transcendentals=0
        ),
    )(grad, clip, master, one, two, rest_grad, rest_master, rest_one, rest_two)


def shards(
    symbol_codes,
    aligned_validity,
    pair_update_cotangent,
    aligned_feature_adjoint,
    local_master_weights,
    local_first_moment,
    local_second_moment,
    remaining_master_weights,
    remaining_first_moment,
    remaining_second_moment,
    remaining_gradient,
):
    gradient, clip = gradients(
        jnp.transpose(symbol_codes[0]),
        jnp.transpose(aligned_validity[0]),
        pair_update_cotangent.reshape(RES * LENGTH, 128),
        aligned_feature_adjoint.reshape(DEPTH * RES, FEATURE_WIDTH),
        local_master_weights,
        remaining_gradient,
    )
    return updates(
        gradient.reshape(-1),
        clip,
        local_master_weights,
        local_first_moment,
        local_second_moment,
        remaining_gradient,
        remaining_master_weights,
        remaining_first_moment,
        remaining_second_moment,
    )


def solution(mesh):
    return jax.shard_map(
        shards,
        mesh=mesh,
        in_specs=(
            P("dp", None, "dap"),
            P("dp", None, "dap"),
            P("dp", "dap", None, None),
            P("dp", None, "dap", None),
            P(),
            P(),
            P(),
            P(("dp", "dap"), None),
            P(("dp", "dap"), None),
            P(("dp", "dap"), None),
            P(("dp", "dap"), None),
        ),
        out_specs=(
            P(),
            P(),
            P(),
            P(),
            P(("dp", "dap"), None),
            P(("dp", "dap"), None),
            P(("dp", "dap"), None),
            P(("dp", "dap"), None),
        ),
        check_vma=False,
    )
```

```python
import jax
import jax.numpy as jnp
from jax import lax
from jax.experimental import pallas as pl
from jax.experimental.pallas import tpu as pltpu
from jax.sharding import PartitionSpec as P

FEATURE_WIDTH = 256
OUTER_LATENT = 32
SYMBOL_KINDS = 23
STEP = 10
PARAMS = 154048
ROWS = 1208
KINDS = 24
MASKED = 24.0
DEPTH = 128
RES = 16
LENGTH = 256
PLANE = 32
RINGS = 8
CROP = 16

PAIR_ROWS = 2 * KINDS
PAIR_BLOCKS = KINDS // 2
WIDE_ROWS = 32
BLOCKS = PAIR_BLOCKS + 2
CHUNKS = 4

beta_first = 0.9
beta_second = 0.999
adam_eps = 1e-06
learn_rate = 0.001
clip_norm = 0.1
norm_eps = 1e-05

MESH = pl.DeviceIdType.MESH
F32 = jnp.float32
BF16 = jnp.bfloat16


def ring_hops(step, size):
    return min(step, size - step)


PLANE_STEPS = sorted(
    (-ring_hops(dx, 4) - ring_hops(dy, 4), dx, dy, dc)
    for dx in range(4)
    for dy in range(4)
    for dc in range(2)
    if dx + dy + dc > 0
)
RING_STEPS = sorted(range(1, RINGS), key=lambda s: -ring_hops(s, RINGS))
CROP_STEPS = sorted(
    (-ring_hops(dz, RINGS) - 2 * dx, dx, dz)
    for dz in range(RINGS)
    for dx in range(2)
    if dz + dx > 0
)
NEAR = CROP // 2
CHUNK = NEAR * RES


def iota(shape, axis):
    return lax.broadcasted_iota(jnp.int32, shape, axis)


def dot(a, b):
    return jnp.dot(a, b, preferred_element_type=F32)


def dot_nt(a, b):
    return lax.dot_general(a, b, (((1,), (1,)), ((), ())), preferred_element_type=F32)


def dot_tn(a, b):
    return lax.dot_general(a, b, (((0,), (0,)), ((), ())), preferred_element_type=F32)


def halves(x):
    high = x.astype(BF16)
    return high, (x - high.astype(F32)).astype(BF16)


def halves_f32(x):
    high = x.astype(BF16).astype(F32)
    return high, x - high


def kernel(
    tok_hbm,
    valid_hbm,
    pair_hbm,
    adj_hbm,
    w_hbm,
    rest_hbm,
    grad_ref,
    clip_ref,
    tok_v,
    valid_v,
    pair_v,
    adj_v,
    w_v,
    rest_v,
    codes,
    counts,
    pair_part,
    pair_recv,
    pair_ring,
    pair_total,
    wide_part,
    wide_recv,
    wide_ring,
    wide_total,
    outer_high,
    outer_low,
    fold_left,
    fold_right,
    shifted,
    wide,
    w_out_v,
    mixed,
    pair_rows,
    normed_twice,
    local_sem,
    block_sem,
    code_send,
    code_recv,
    plane_send,
    plane_recv,
    ring_send,
    ring_recv,
    all_send,
    all_recv,
):
    dp = lax.axis_index("dp")
    dap = lax.axis_index("dap")
    z = lax.div(dap, 2)
    x_hi = lax.rem(dap, 2)
    core = lax.rem(dp, 2)
    y = lax.rem(lax.div(dp, 2), 4)
    x = x_hi * 2 + lax.div(dp, 8)

    xs = [lax.rem(x + dx, 4) for dx in range(4)]
    xs = [(lax.rem(value, 2) * 8, lax.div(value, 2)) for value in xs]
    ys = [lax.rem(y + dy, 4) * 2 for dy in range(4)]
    cores = [lax.rem(core + dc, 2) for dc in range(2)]

    def in_plane(dx, dy, dc):
        low, high = xs[dx]
        return cores[dc] * 16 + low + ys[dy] + high, (low + ys[dy] + cores[dc], z * 2 + high)

    slot = in_plane(0, 0, 0)[0]
    peers = [in_plane(*step[1:]) for step in PLANE_STEPS]
    zs = [lax.rem(z + dz, RINGS) * 2 for dz in range(RINGS)]
    mates = [zs[dz] + (1 - x_hi if dx else x_hi) for _, dx, dz in CROP_STEPS]
    order = [dap] + mates[::-1]

    loads = []
    for n, (src, dst) in enumerate(
        (
            (tok_hbm, tok_v),
            (valid_hbm, valid_v),
            (w_hbm, w_v),
            (adj_hbm, adj_v),
            (rest_hbm, rest_v),
        )
    ):
        copy = pltpu.make_async_copy(src, dst, local_sem.at[n])
        copy.start()
        loads.append(copy)

    barrier = pltpu.get_barrier_semaphore()
    greetings = [(step[0], (dp, mate)) for step, mate in zip(CROP_STEPS, mates)]
    greetings += [(step[0], peer) for step, (_, peer) in zip(PLANE_STEPS, peers)]
    for _, device in sorted(greetings, key=lambda pair: pair[0]):
        pl.semaphore_signal(barrier, inc=1, device_id=device, device_id_type=MESH)

    for n, block in enumerate(order):
        copy = pltpu.make_async_copy(
            pair_hbm.at[:, block],
            pair_v.at[n // NEAR, :, pl.ds(n % NEAR * RES, RES)],
            block_sem.at[n],
        )
        copy.start()
        loads.append(copy)

    loads[0].wait()
    loads[1].wait()
    tok = tok_v[...].astype(F32)
    own = jnp.where(valid_v[...] != 0, tok, MASKED)
    codes[dap] = own.astype(BF16)
    pl.semaphore_wait(barrier, CROP - 1 + PLANE - 1)

    def wait_all(ref, sem):
        pltpu.make_async_copy(ref, ref, sem).wait()

    for n, mate in enumerate(mates):
        pltpu.make_async_remote_copy(
            src_ref=codes.at[dap],
            dst_ref=codes.at[dap],
            send_sem=code_send,
            recv_sem=code_recv.at[0 if n >= CROP - NEAR else 1],
            device_id=(dp, mate),
            device_id_type=MESH,
        ).start()

    spread = (iota((RES, 128), 1) % RES == iota((RES, 128), 0)).astype(F32)
    tiled = dot_tn(tok, spread)
    tiled = jnp.where(iota((DEPTH, 128), 0) % 8 == iota((DEPTH, 128), 1) // RES, tiled, 0.0)
    gather = (iota((RES, DEPTH), 1) // 8 == iota((RES, DEPTH), 0)).astype(F32)
    flat = dot(gather, tiled)
    kind = iota((KINDS, 128), 0).astype(F32)
    hot = jnp.concatenate(
        [(flat[q : q + 1, :] == kind).astype(F32) for q in range(RES)], axis=1
    ).astype(BF16)
    loads[3].wait()
    feat = dot(hot, adj_v[...])
    loads[4].wait()
    rest = rest_v[...]
    square = jnp.sum((rest * rest).reshape(32, 8, 512), axis=0)
    square = square[:, :128] + square[:, 128:256] + square[:, 256:384] + square[:, 384:]
    for copy in loads[5:]:
        copy.wait()
    pair_sum = dot(
        jnp.ones((16, RES * LENGTH), BF16), pair_v[...].reshape(RES * LENGTH, 128)
    )
    wide_part[0] = jnp.concatenate([feat[:, :128], pair_sum[:8]], axis=0)
    wide_part[1] = jnp.concatenate([feat[:, 128:], square], axis=0)

    def owner_of(p):
        return ((p % 16 // 2) * 2 + p // 16, z * 2 + p % 2)

    def plane_copy(part, recv, block, target):
        return pltpu.make_async_remote_copy(
            src_ref=part.at[block],
            dst_ref=recv.at[slot],
            send_sem=plane_send.at[0 if part is pair_part else 1],
            recv_sem=plane_recv,
            device_id=owner_of(target),
            device_id_type=MESH,
        )

    def to_owners(part, recv, first):
        for block in range(part.shape[0]):

            @pl.when(slot != first + block)
            def _():
                plane_copy(part, recv, block, first + block).start()

    def owns_pair(then):
        pl.when(slot < PAIR_BLOCKS)(then)

    def owns_wide(then):
        pl.when((slot >= PAIR_BLOCKS) & (slot < BLOCKS))(then)

    to_owners(wide_part, wide_recv, PAIR_BLOCKS)

    loads[2].wait()
    weights = jnp.concatenate(
        [
            w_v[pl.ds(0, 153600)].reshape(1200, 128),
            jnp.concatenate(
                [w_v[pl.ds(153600, PARAMS - 153600)], jnp.zeros((ROWS * 128 - PARAMS,), F32)]
            ).reshape(8, 128),
        ],
        axis=0,
    )
    weights = weights.astype(BF16).astype(F32)
    low_lane = iota((1, 128), 1) < 64
    shifted[0:ROWS] = pltpu.roll(weights, 64, 1)
    w_out_v[...] = jnp.where(
        low_lane, shifted[pl.ds(132, 1024), :], shifted[pl.ds(133, 1024), :]
    )
    first = jnp.where(
        low_lane,
        shifted[pl.ds(1157, KINDS, stride=2), :],
        shifted[pl.ds(1158, KINDS, stride=2), :],
    )
    second = jnp.where(
        low_lane,
        shifted[pl.ds(1158, KINDS, stride=2), :],
        shifted[pl.ds(1159, KINDS, stride=2), :],
    )
    table = jnp.concatenate([first, second], axis=1)
    table = jnp.where(iota((KINDS, FEATURE_WIDTH), 0) < SYMBOL_KINDS, table, 0.0)
    center = jnp.mean(table, axis=1, keepdims=True)
    variance = jnp.mean((table - center) ** 2, axis=1, keepdims=True)
    inverse = lax.rsqrt(variance + norm_eps)
    unit = (table - center) * inverse
    gain = jnp.concatenate([weights[0:1], weights[1:2]], axis=1)
    shift = jnp.concatenate([weights[2:3], weights[3:4]], axis=1)
    normed = (unit * gain + shift).astype(BF16).astype(F32)
    w_rows = weights[4:132]
    pair_rows[pl.ds(0, 128, stride=2), :] = jnp.where(low_lane, w_rows, 0.0)
    pair_rows[pl.ds(1, 128, stride=2), :] = jnp.where(low_lane, pltpu.roll(w_rows, 64, 1), 0.0)
    w_pair = pair_rows[...]
    bias = jnp.where(low_lane, weights[132:133], 0.0)
    acts = (dot(normed, w_pair) + bias).astype(BF16).astype(F32)
    acts = jnp.where(iota((KINDS, 128), 0) < SYMBOL_KINDS, acts, 0.0)

    normed_twice[...] = jnp.transpose(jnp.concatenate([normed, normed], axis=0)).astype(BF16)

    he_row = iota((1024, 128), 0)
    lane = iota((1024, 128), 1)
    tile_u = jnp.concatenate([acts] * KINDS, axis=0)
    tile_v = jnp.concatenate(
        [jnp.broadcast_to(acts[v : v + 1], (KINDS, 128)) for v in range(KINDS)], axis=0
    )
    outer = dot_nt((he_row // 32 == lane).astype(F32), tile_u) * (1.0 / DEPTH)
    outer = outer * dot_nt((he_row % 32 == lane - 32).astype(F32), tile_v)
    outer_hi, outer_lo = halves(outer)
    outer_high[...] = outer_hi
    outer_low[...] = outer_lo

    def mix(weights, blocks, fold, first_row):
        blocks = jnp.concatenate(blocks, axis=1).astype(BF16)
        mixes = dot(weights.astype(BF16), blocks) * (1.0 / DEPTH)
        for h in range(OUTER_LATENT):
            mixed[pl.ds(h, KINDS, stride=32), :] = mixes[:, h * 128 : (h + 1) * 128]
        turned = jnp.concatenate([mixed[v * 32 : (v + 1) * 32] for v in range(KINDS)], axis=1)
        high, low = halves_f32(turned)
        none = jnp.zeros((OUTER_LATENT, KINDS * 128), F32)
        if first_row == 0:
            rows = [high, none, low, none]
        else:
            rows = [none, high, none, low]
        fold[...] = jnp.transpose(jnp.concatenate(rows, axis=0)).astype(BF16)

    mix(
        acts[:, OUTER_LATENT : 2 * OUTER_LATENT],
        [w_out_v[h * 32 : (h + 1) * 32] for h in range(OUTER_LATENT)],
        fold_left,
        0,
    )
    mix(
        acts[:, :OUTER_LATENT],
        [w_out_v[pl.ds(e, 32, stride=32), :] for e in range(OUTER_LATENT)],
        fold_right,
        1,
    )

    hot_own = jnp.concatenate(
        [(own[i : i + 1, :] == kind).astype(F32) for i in range(RES)], axis=0
    ).astype(BF16)

    for half in range(2):
        wait_all(codes.at[pl.ds(0, NEAR - 1 if half == 0 else CROP - NEAR)], code_recv.at[half])
        every = jnp.concatenate(
            [codes[block].astype(F32) for block in order[half * NEAR : (half + 1) * NEAR]], axis=0
        )
        every = jnp.transpose(every)
        for p in range(PAIR_BLOCKS):
            hot_all = jnp.concatenate(
                [(every == float(v)).astype(F32) for v in (2 * p, 2 * p + 1)], axis=1
            )
            both = dot(hot_own, hot_all.astype(BF16)).reshape(RES, KINDS, 2 * CHUNK)
            both = jnp.concatenate([both[:, :, :CHUNK], both[:, :, CHUNK:]], axis=1).astype(BF16)
            for i in range(RES):
                counts[
                    half, p * PAIR_ROWS : (p + 1) * PAIR_ROWS, i * CHUNK : (i + 1) * CHUNK
                ] = both[i]
        part_sums = dot(counts[half], pair_v[half].reshape(RES * CHUNK, 128))
        sums = part_sums if half == 0 else sums + part_sums
    pair_part[...] = sums.astype(BF16).reshape(PAIR_BLOCKS, PAIR_ROWS, 128)
    to_owners(pair_part, pair_recv, 0)

    def reduce(block, part, recv, ring, total, others):
        recv[slot] = part[block]
        wait_all(recv.at[pl.ds(0, PLANE - 1)], plane_recv)
        ring[z] = jnp.sum(recv[...].astype(F32), axis=0).astype(ring.dtype)
        for step in RING_STEPS:
            pltpu.make_async_remote_copy(
                src_ref=ring.at[z],
                dst_ref=ring.at[z],
                send_sem=ring_send,
                recv_sem=ring_recv,
                device_id=(dp, zs[step] + x_hi),
                device_id_type=MESH,
            ).start()
        wait_all(ring.at[pl.ds(0, RINGS - 1)], ring_recv)
        total[block] = jnp.sum(ring[...].astype(F32), axis=0).astype(total.dtype)
        for _, peer in peers:
            pltpu.make_async_remote_copy(
                src_ref=total.at[block],
                dst_ref=total.at[block],
                send_sem=all_send,
                recv_sem=all_recv.at[others],
                device_id=peer,
                device_id_type=MESH,
            ).start()

    @owns_pair
    def _():
        reduce(slot, pair_part, pair_recv, pair_ring, pair_total, 0)
        wait_all(pair_total.at[pl.ds(0, PAIR_BLOCKS - 1)], all_recv.at[0])
        wait_all(wide_total, all_recv.at[1])

    @owns_wide
    def _():
        reduce(slot - PAIR_BLOCKS, wide_part, wide_recv, wide_ring, wide_total, 1)
        wait_all(pair_total, all_recv.at[0])
        wait_all(wide_total.at[pl.ds(0, 1)], all_recv.at[1])

    @pl.when(slot >= BLOCKS)
    def _():
        wait_all(pair_total, all_recv.at[0])
        wait_all(wide_total, all_recv.at[1])

    summed = pair_total[...].reshape(KINDS * KINDS, 128)
    mixed[0 : KINDS * KINDS] = summed.astype(F32)
    by_first = jnp.concatenate([mixed[v * KINDS : (v + 1) * KINDS] for v in range(KINDS)], axis=1)
    by_second = jnp.concatenate(
        [mixed[pl.ds(u, KINDS, stride=KINDS), :] for u in range(KINDS)], axis=1
    )
    act = dot(by_first.astype(BF16), fold_left[...]) + dot(by_second.astype(BF16), fold_right[...])
    act = act + pltpu.roll(act, 64, 1)
    act = jnp.where((iota((KINDS, 128), 0) < SYMBOL_KINDS) & low_lane, act, 0.0)
    w_out_grad = dot(outer_high[...], summed) + dot(outer_low[...], summed)
    act_parts = jnp.concatenate(halves_f32(act), axis=0)
    norm_grad = dot_nt(act_parts, w_pair)
    norm_grad = norm_grad[:KINDS] + norm_grad[KINDS:]
    wide[...] = dot(normed_twice[...], act_parts.astype(BF16))
    w_pair_grad = wide[pl.ds(0, 128, stride=2), :] + pltpu.roll(
        wide[pl.ds(1, 128, stride=2), :], 64, 1
    )
    gained = norm_grad * gain
    feat = jnp.concatenate([wide_total[0][:KINDS], wide_total[1][:KINDS]], axis=1)
    table_grad = feat + inverse * (
        gained
        - jnp.mean(gained, axis=1, keepdims=True)
        - unit * jnp.mean(gained * unit, axis=1, keepdims=True)
    )
    gain_grad = jnp.sum(norm_grad * unit, axis=0, keepdims=True)
    shift_grad = jnp.sum(norm_grad, axis=0, keepdims=True)
    bias_grad = jnp.sum(act, axis=0, keepdims=True)

    shifted[0:8] = jnp.zeros((8, 128), F32)
    shifted[8:1032] = pltpu.roll(w_out_grad, 64, 1)
    shifted[1032:1088] = jnp.zeros((56, 128), F32)
    shifted[1032:1033] = pltpu.roll(wide_total[0][KINDS : KINDS + 1], 64, 1)
    shifted[pl.ds(1033, SYMBOL_KINDS, stride=2), :] = pltpu.roll(
        table_grad[:SYMBOL_KINDS, :128], 64, 1
    )
    shifted[pl.ds(1034, SYMBOL_KINDS, stride=2), :] = pltpu.roll(
        table_grad[:SYMBOL_KINDS, 128:], 64, 1
    )
    grad_ref[128:ROWS] = jnp.where(low_lane, shifted[3:1083], shifted[4:1084])
    grad_ref[0:4] = jnp.concatenate(
        [gain_grad[:, :128], gain_grad[:, 128:], shift_grad[:, :128], shift_grad[:, 128:]], axis=0
    )
    grad_ref[4:132] = w_pair_grad
    grad_ref[132:133] = jnp.where(low_lane, bias_grad, grad_ref[132:133])
    grad = grad_ref[...]
    squares = jnp.sum((grad * grad).reshape(ROWS // 8, 8, 128), axis=0)
    norm = jnp.sum(squares + wide_total[1][KINDS:])
    norm = jnp.sqrt(jnp.full((1, 512), norm, F32))
    clip_ref[...] = jnp.minimum(1.0, clip_norm / (norm + 1e-06))

    wait_all(codes.at[pl.ds(0, CROP - 1)], code_send)

    def finish(recv, ring, pairs, wides):
        wait_all(pair_part.at[pl.ds(0, pairs)], plane_send.at[0])
        wait_all(wide_part.at[pl.ds(0, wides)], plane_send.at[1])
        if recv is not None:
            wait_all(ring.at[pl.ds(0, RINGS - 1)], ring_send)
            wait_all(recv.at[pl.ds(0, PLANE - 1)], all_send)

    @owns_pair
    def _():
        finish(pair_recv, pair_ring, PAIR_BLOCKS - 1, 2)

    @owns_wide
    def _():
        finish(wide_recv, wide_ring, PAIR_BLOCKS, 1)

    @pl.when(slot >= BLOCKS)
    def _():
        finish(None, None, PAIR_BLOCKS, 2)


def in_hbm(array):
    return pltpu.with_memory_space_constraint(array, pltpu.HBM)


def gradients(*arrays):
    return pl.pallas_call(
        kernel,
        out_shape=(
            jax.ShapeDtypeStruct((ROWS, 128), F32),
            jax.ShapeDtypeStruct((1, 512), F32),
        ),
        in_specs=[pl.BlockSpec(memory_space=pltpu.HBM)] * 6,
        out_specs=(
            pl.BlockSpec(memory_space=pltpu.VMEM),
            pl.BlockSpec(memory_space=pltpu.VMEM),
        ),
        scratch_shapes=[
            pltpu.VMEM((RES, DEPTH), jnp.int32),
            pltpu.VMEM((RES, DEPTH), jnp.int32),
            pltpu.VMEM((2, RES, CHUNK, 128), BF16),
            pltpu.VMEM((DEPTH * RES, FEATURE_WIDTH), BF16),
            pltpu.VMEM((PARAMS,), F32),
            pltpu.VMEM((256, 512), F32),
            pltpu.VMEM((CROP, RES, DEPTH), BF16),
            pltpu.VMEM((2, KINDS * KINDS, RES * CHUNK), BF16),
            pltpu.VMEM((PAIR_BLOCKS, PAIR_ROWS, 128), BF16),
            pltpu.VMEM((PLANE, PAIR_ROWS, 128), BF16),
            pltpu.VMEM((RINGS, PAIR_ROWS, 128), BF16),
            pltpu.VMEM((PAIR_BLOCKS, PAIR_ROWS, 128), BF16),
            pltpu.VMEM((2, WIDE_ROWS, 128), F32),
            pltpu.VMEM((PLANE, WIDE_ROWS, 128), F32),
            pltpu.VMEM((RINGS, WIDE_ROWS, 128), F32),
            pltpu.VMEM((2, WIDE_ROWS, 128), F32),
            pltpu.VMEM((1024, KINDS * KINDS), BF16),
            pltpu.VMEM((1024, KINDS * KINDS), BF16),
            pltpu.VMEM((KINDS * 128, 128), BF16),
            pltpu.VMEM((KINDS * 128, 128), BF16),
            pltpu.VMEM((ROWS + 8, 128), F32),
            pltpu.VMEM((FEATURE_WIDTH, 128), F32),
            pltpu.VMEM((1024, 128), F32),
            pltpu.VMEM((KINDS * 32, 128), F32),
            pltpu.VMEM((FEATURE_WIDTH, 128), F32),
            pltpu.VMEM((FEATURE_WIDTH, 2 * KINDS), BF16),
            pltpu.SemaphoreType.DMA((5,)),
            pltpu.SemaphoreType.DMA((CROP,)),
            pltpu.SemaphoreType.DMA,
            pltpu.SemaphoreType.DMA((2,)),
            pltpu.SemaphoreType.DMA((2,)),
            pltpu.SemaphoreType.DMA,
            pltpu.SemaphoreType.DMA,
            pltpu.SemaphoreType.DMA,
            pltpu.SemaphoreType.DMA,
            pltpu.SemaphoreType.DMA((2,)),
        ],
        compiler_params=pltpu.CompilerParams(
            collective_id=0, has_side_effects=True, vmem_limit_bytes=40 * 1024 * 1024
        ),
        cost_estimate=pl.CostEstimate(
            flops=3_000_000_000, bytes_accessed=40_000_000, transcendentals=0
        ),
    )(*[in_hbm(array) for array in arrays])


def adam_update(master, moment_one, moment_two, scaled):
    first = beta_first * moment_one + (1.0 - beta_first) * scaled
    second = beta_second * moment_two + (1.0 - beta_second) * scaled * scaled
    fix_first = 1.0 - beta_first**STEP
    fix_second = 1.0 - beta_second**STEP
    update = first * (learn_rate / fix_first) / (jnp.sqrt(second * (1.0 / fix_second)) + adam_eps)
    return (master - update, first, second)


def update_kernel(
    grad_ref,
    clip_ref,
    master_ref,
    one_ref,
    two_ref,
    rest_grad_ref,
    rest_master_ref,
    rest_one_ref,
    rest_two_ref,
    *refs,
):
    outs, held, sems = refs[:8], refs[8:16], refs[16]
    clip = clip_ref[...]
    rest_step = rest_grad_ref.shape[0] // CHUNKS
    flat_step = 1024 * 38
    copies = []

    def send(n, where):
        copy = pltpu.make_async_copy(held[n].at[where], outs[n].at[where], sems.at[len(copies)])
        copy.start()
        copies.append(copy)

    for chunk in range(CHUNKS):
        where = pl.ds(chunk * rest_step, rest_step)
        new = adam_update(
            rest_master_ref[where], rest_one_ref[where], rest_two_ref[where], rest_grad_ref[where] * clip
        )
        for n, value in enumerate(new + (new[0],)):
            held[4 + n][where] = value.astype(held[4 + n].dtype)
            send(4 + n, where)
    factor = jnp.max(clip)
    for chunk in range(CHUNKS):
        start = chunk * flat_step
        where = pl.ds(start, min(flat_step, PARAMS - start))
        new = adam_update(master_ref[where], one_ref[where], two_ref[where], grad_ref[where] * factor)
        for n, value in enumerate(new + (new[0],)):
            held[n][where] = value.astype(held[n].dtype)
            send(n, where)
    for copy in copies:
        copy.wait()


def updates(grad, clip, master, one, two, rest_grad, rest_master, rest_one, rest_two):
    flat = [jax.ShapeDtypeStruct(master.shape, dtype) for dtype in (F32, F32, F32, BF16)]
    rows = [jax.ShapeDtypeStruct(rest_master.shape, dtype) for dtype in (F32, F32, F32, BF16)]
    return pl.pallas_call(
        update_kernel,
        out_shape=tuple(flat + rows),
        in_specs=[pl.BlockSpec(memory_space=pltpu.VMEM)] * 9,
        out_specs=tuple([pl.BlockSpec(memory_space=pltpu.HBM)] * 8),
        scratch_shapes=[pltpu.VMEM(out.shape, out.dtype) for out in flat + rows]
        + [pltpu.SemaphoreType.DMA((8 * CHUNKS,))],
        compiler_params=pltpu.CompilerParams(vmem_limit_bytes=20 * 1024 * 1024),
        cost_estimate=pl.CostEstimate(
            flops=5_000_000, bytes_accessed=8_000_000, transcendentals=0
        ),
    )(grad, clip, master, one, two, rest_grad, rest_master, rest_one, rest_two)


def shards(
    symbol_codes,
    aligned_validity,
    pair_update_cotangent,
    aligned_feature_adjoint,
    local_master_weights,
    local_first_moment,
    local_second_moment,
    remaining_master_weights,
    remaining_first_moment,
    remaining_second_moment,
    remaining_gradient,
):
    gradient, clip = gradients(
        jnp.transpose(symbol_codes[0]),
        jnp.transpose(aligned_validity[0]),
        pair_update_cotangent.reshape(RES, CROP, RES, 128),
        aligned_feature_adjoint.reshape(DEPTH * RES, FEATURE_WIDTH),
        local_master_weights,
        remaining_gradient,
    )
    return updates(
        gradient.reshape(-1),
        clip,
        local_master_weights,
        local_first_moment,
        local_second_moment,
        remaining_gradient,
        remaining_master_weights,
        remaining_first_moment,
        remaining_second_moment,
    )


def solution(mesh):
    return jax.shard_map(
        shards,
        mesh=mesh,
        in_specs=(
            P("dp", None, "dap"),
            P("dp", None, "dap"),
            P("dp", "dap", None, None),
            P("dp", None, "dap", None),
            P(),
            P(),
            P(),
            P(("dp", "dap"), None),
            P(("dp", "dap"), None),
            P(("dp", "dap"), None),
            P(("dp", "dap"), None),
        ),
        out_specs=(
            P(),
            P(),
            P(),
            P(),
            P(("dp", "dap"), None),
            P(("dp", "dap"), None),
            P(("dp", "dap"), None),
            P(("dp", "dap"), None),
        ),
        check_vma=False,
    )
```

```python
import jax
import jax.numpy as jnp
from jax import lax
from jax.experimental import pallas as pl
from jax.experimental.pallas import tpu as pltpu
from jax.sharding import PartitionSpec as P

FEATURE_WIDTH = 256
OUTER_LATENT = 32
SYMBOL_KINDS = 23
STEP = 10
PARAMS = 154048
ROWS = 1208
KINDS = 24
MASKED = 24.0
DEPTH = 128
RES = 16
LENGTH = 256
PLANE = 32
RINGS = 8
CROP = 16

PAIR_ROWS = 2 * KINDS
PAIR_BLOCKS = KINDS // 2
WIDE_ROWS = 32
BLOCKS = PAIR_BLOCKS + 2
CHUNKS = 8

beta_first = 0.9
beta_second = 0.999
adam_eps = 1e-06
learn_rate = 0.001
clip_norm = 0.1
norm_eps = 1e-05

MESH = pl.DeviceIdType.MESH
F32 = jnp.float32
BF16 = jnp.bfloat16
F8 = jnp.float8_e4m3fn


def ring_hops(step, size):
    return min(step, size - step)


PLANE_STEPS = sorted(
    (-ring_hops(dx, 4) - ring_hops(dy, 4), dx, dy, dc)
    for dx in range(4)
    for dy in range(4)
    for dc in range(2)
    if dx + dy + dc > 0
)
RING_STEPS = sorted(range(1, RINGS), key=lambda s: -ring_hops(s, RINGS))
CROP_STEPS = sorted(
    (-ring_hops(dz, RINGS) - 2 * dx, dx, dz)
    for dz in range(RINGS)
    for dx in range(2)
    if dz + dx > 0
)
FIRST = 10
STAGES = ((0, 8), (8, 12), (12, 16))


def iota(shape, axis):
    return lax.broadcasted_iota(jnp.int32, shape, axis)


def dot(a, b):
    return jnp.dot(a, b, preferred_element_type=F32)


def dot_nt(a, b):
    return lax.dot_general(a, b, (((1,), (1,)), ((), ())), preferred_element_type=F32)


def dot_tn(a, b):
    return lax.dot_general(a, b, (((0,), (0,)), ((), ())), preferred_element_type=F32)


def halves_f32(x):
    high = x.astype(BF16).astype(F32)
    return high, x - high


def kernel(
    tok_hbm,
    valid_hbm,
    pair_hbm,
    adj_hbm,
    w_hbm,
    rest_hbm,
    grad_ref,
    clip_ref,
    tok_v,
    valid_v,
    pair_near,
    pair_middle,
    pair_far,
    adj_v,
    w_v,
    rest_v,
    codes,
    counts_near,
    counts_middle,
    counts_far,
    pair_part,
    pair_recv,
    pair_ring,
    pair_total,
    wide_part,
    wide_recv,
    wide_ring,
    wide_total,
    outer_v,
    fold,
    shifted,
    wide,
    w_out_v,
    mixed,
    pair_rows,
    pair_turned,
    normed_twice,
    local_sem,
    block_sem,
    code_send,
    code_recv,
    plane_send,
    plane_recv,
    ring_send,
    ring_recv,
    all_send,
    all_recv,
):
    dp = lax.axis_index("dp")
    dap = lax.axis_index("dap")
    z = lax.div(dap, 2)
    x_hi = lax.rem(dap, 2)
    core = lax.rem(dp, 2)
    y = lax.rem(lax.div(dp, 2), 4)
    x = x_hi * 2 + lax.div(dp, 8)

    xs = [lax.rem(x + dx, 4) for dx in range(4)]
    xs = [(lax.rem(value, 2) * 8, lax.div(value, 2)) for value in xs]
    ys = [lax.rem(y + dy, 4) * 2 for dy in range(4)]
    cores = [lax.rem(core + dc, 2) for dc in range(2)]

    def in_plane(dx, dy, dc):
        low, high = xs[dx]
        return cores[dc] * 16 + low + ys[dy] + high, (low + ys[dy] + cores[dc], z * 2 + high)

    slot = in_plane(0, 0, 0)[0]
    peers = [in_plane(*step[1:]) for step in PLANE_STEPS]
    zs = [lax.rem(z + dz, RINGS) * 2 for dz in range(RINGS)]
    mates = [zs[dz] + (1 - x_hi if dx else x_hi) for _, dx, dz in CROP_STEPS]
    order = [dap] + mates[::-1]

    barrier = pltpu.get_barrier_semaphore()
    greetings = [(step[0], (dp, mate)) for step, mate in zip(CROP_STEPS, mates)]
    greetings += [(step[0], peer) for step, (_, peer) in zip(PLANE_STEPS, peers)]
    greetings = [device for _, device in sorted(greetings, key=lambda pair: pair[0])]
    for device in greetings[:FIRST]:
        pl.semaphore_signal(barrier, inc=1, device_id=device, device_id_type=MESH)


    loads = []
    for n, (src, dst) in enumerate(
        (
            (tok_hbm, tok_v),
            (valid_hbm, valid_v),
            (w_hbm, w_v),
            (adj_hbm, adj_v),
            (rest_hbm, rest_v),
        )
    ):
        copy = pltpu.make_async_copy(src, dst, local_sem.at[n])
        copy.start()
        loads.append(copy)

    for device in greetings[FIRST:]:
        pl.semaphore_signal(barrier, inc=1, device_id=device, device_id_type=MESH)

    cotangents = (pair_near, pair_middle, pair_far)
    for stage, (start, stop) in enumerate(STAGES):
        for n in range(start, stop):
            copy = pltpu.make_async_copy(
                pair_hbm.at[:, order[n]],
                cotangents[stage].at[:, pl.ds((n - start) * RES, RES)],
                block_sem.at[n],
            )
            copy.start()
            loads.append(copy)

    loads[0].wait()
    loads[1].wait()
    tok = tok_v[...].astype(F32)
    own = jnp.where(valid_v[...] != 0, tok, MASKED)
    codes[dap] = own.astype(BF16)
    pl.semaphore_wait(barrier, CROP - 1 + PLANE - 1)

    def wait_all(ref, sem):
        pltpu.make_async_copy(ref, ref, sem).wait()

    for n in range(CROP - 1, 0, -1):
        pltpu.make_async_remote_copy(
            src_ref=codes.at[dap],
            dst_ref=codes.at[dap],
            send_sem=code_send,
            recv_sem=code_recv.at[[start <= n < stop for start, stop in STAGES].index(True)],
            device_id=(dp, order[n]),
            device_id_type=MESH,
        ).start()

    spread = (iota((RES, 128), 1) % RES == iota((RES, 128), 0)).astype(F32)
    tiled = dot_tn(tok, spread)
    tiled = jnp.where(iota((DEPTH, 128), 0) % 8 == iota((DEPTH, 128), 1) // RES, tiled, 0.0)
    gather = (iota((RES, DEPTH), 1) // 8 == iota((RES, DEPTH), 0)).astype(F32)
    flat = dot(gather, tiled)
    kind = iota((KINDS, 128), 0).astype(F32)
    hot = jnp.concatenate(
        [(flat[q : q + 1, :] == kind).astype(F32) for q in range(RES)], axis=1
    ).astype(BF16)
    loads[3].wait()
    feat = dot(hot, adj_v[...])
    loads[4].wait()
    rest = rest_v[...]
    square = jnp.sum((rest * rest).reshape(32, 8, 512), axis=0)
    square = square[:, :128] + square[:, 128:256] + square[:, 256:384] + square[:, 384:]
    for copy in loads[5:]:
        copy.wait()
    pair_sum = jnp.zeros((16, 128), F32)
    for cotangent in cotangents:
        rows = cotangent.shape[0] * cotangent.shape[1]
        pair_sum = pair_sum + dot(jnp.ones((16, rows), BF16), cotangent[...].reshape(rows, 128))
    wide_part[0] = jnp.concatenate([feat[:, :128], pair_sum[:8]], axis=0)
    wide_part[1] = jnp.concatenate([feat[:, 128:], square], axis=0)

    def owner_of(p):
        return ((p % 16 // 2) * 2 + p // 16, z * 2 + p % 2)

    def plane_copy(part, recv, block, target):
        return pltpu.make_async_remote_copy(
            src_ref=part.at[block],
            dst_ref=recv.at[slot],
            send_sem=plane_send.at[0 if part is pair_part else 1],
            recv_sem=plane_recv,
            device_id=owner_of(target),
            device_id_type=MESH,
        )

    def to_owners(part, recv, first):
        for block in range(part.shape[0]):

            @pl.when(slot != first + block)
            def _():
                plane_copy(part, recv, block, first + block).start()

    def owns_pair(then):
        pl.when(slot < PAIR_BLOCKS)(then)

    def owns_wide(then):
        pl.when((slot >= PAIR_BLOCKS) & (slot < BLOCKS))(then)

    to_owners(wide_part, wide_recv, PAIR_BLOCKS)

    loads[2].wait()
    weights = jnp.concatenate(
        [
            w_v[pl.ds(0, 153600)].reshape(1200, 128),
            jnp.concatenate(
                [w_v[pl.ds(153600, PARAMS - 153600)], jnp.zeros((ROWS * 128 - PARAMS,), F32)]
            ).reshape(8, 128),
        ],
        axis=0,
    )
    weights = weights.astype(BF16).astype(F32)
    low_lane = iota((1, 128), 1) < 64
    shifted[0:ROWS] = pltpu.roll(weights, 64, 1)
    w_out_v[...] = jnp.where(
        low_lane, shifted[pl.ds(132, 1024), :], shifted[pl.ds(133, 1024), :]
    )
    first = jnp.where(
        low_lane,
        shifted[pl.ds(1157, KINDS, stride=2), :],
        shifted[pl.ds(1158, KINDS, stride=2), :],
    )
    second = jnp.where(
        low_lane,
        shifted[pl.ds(1158, KINDS, stride=2), :],
        shifted[pl.ds(1159, KINDS, stride=2), :],
    )
    table = jnp.concatenate([first, second], axis=1)
    table = jnp.where(iota((KINDS, FEATURE_WIDTH), 0) < SYMBOL_KINDS, table, 0.0)
    center = jnp.mean(table, axis=1, keepdims=True)
    variance = jnp.mean((table - center) ** 2, axis=1, keepdims=True)
    inverse = lax.rsqrt(variance + norm_eps)
    unit = (table - center) * inverse
    gain = jnp.concatenate([weights[0:1], weights[1:2]], axis=1)
    shift = jnp.concatenate([weights[2:3], weights[3:4]], axis=1)
    normed = (unit * gain + shift).astype(BF16).astype(F32)
    w_rows = weights[4:132]
    pair_rows[pl.ds(0, 128, stride=2), :] = jnp.where(low_lane, w_rows, 0.0)
    pair_rows[pl.ds(1, 128, stride=2), :] = jnp.where(low_lane, pltpu.roll(w_rows, 64, 1), 0.0)
    w_pair = pair_rows[...]
    pair_turned[...] = jnp.transpose(w_pair).astype(BF16)
    bias = jnp.where(low_lane, weights[132:133], 0.0)
    acts = (dot(normed, w_pair) + bias).astype(BF16).astype(F32)
    acts = jnp.where(iota((KINDS, 128), 0) < SYMBOL_KINDS, acts, 0.0)

    normed_twice[...] = jnp.transpose(jnp.concatenate([normed, normed], axis=0)).astype(BF16)

    hot_own = jnp.concatenate(
        [(own[i : i + 1, :] == kind).astype(F32) for i in range(RES)], axis=0
    ).astype(F8)

    sums = jnp.zeros((KINDS * KINDS, 128), F32)
    for stage, (start, stop) in enumerate(STAGES):
        wait_all(codes.at[pl.ds(0, stop - max(start, 1))], code_recv.at[stage])
        every = jnp.concatenate([codes[block].astype(F32) for block in order[start:stop]], axis=0)
        every = jnp.transpose(every)
        size = (stop - start) * RES
        counts = (counts_near, counts_middle, counts_far)[stage]
        count = 256 // size
        for first in range(0, KINDS, count):
            hot_all = jnp.concatenate(
                [(every == float(v)).astype(F32) for v in range(first, first + count)], axis=1
            )
            all_pairs = dot(hot_own, hot_all.astype(F8))
            for p in range(first // 2, (first + count) // 2):
                if size == 128:
                    both = all_pairs.reshape(RES, KINDS, 256)
                    both = jnp.concatenate([both[:, :, :128], both[:, :, 128:]], axis=1)
                else:
                    start_lane = (p - first // 2) * 128
                    both = all_pairs[:, start_lane : start_lane + 128]
                    turned = pltpu.roll(both, 64, 1).reshape(RES // 2, 2, KINDS, 128)
                    both = both.reshape(RES // 2, 2, KINDS, 128)
                    both = jnp.concatenate(
                        [
                            jnp.where(low_lane, both[:, 0], turned[:, 1]),
                            jnp.where(low_lane, turned[:, 0], both[:, 1]),
                        ],
                        axis=1,
                    )
                both = both.astype(BF16)
                for i in range(both.shape[0]):
                    counts[p * PAIR_ROWS : (p + 1) * PAIR_ROWS, i * 128 : (i + 1) * 128] = both[i]
        sums = sums + dot(counts[...], cotangents[stage][...].reshape(RES * size, 128))
    pair_part[...] = sums.astype(BF16).reshape(PAIR_BLOCKS, PAIR_ROWS, 128)
    to_owners(pair_part, pair_recv, 0)

    he_row = iota((1024, 128), 0)
    lane = iota((1024, 128), 1)
    acts_t = jnp.transpose(acts).astype(BF16)
    left_of = dot((he_row // 32 == lane).astype(F32).astype(BF16), acts_t).astype(BF16)
    right_of = dot((he_row % 32 == lane - 32).astype(F32).astype(BF16), acts_t).astype(BF16)
    uv = iota((KINDS, KINDS * KINDS), 1)
    kind_row = iota((KINDS, KINDS * KINDS), 0)
    outer = dot(left_of, (uv % KINDS == kind_row).astype(F32).astype(BF16)) * (1.0 / DEPTH)
    outer = outer * dot(right_of, (uv // KINDS == kind_row).astype(F32).astype(BF16))
    outer_v[...] = outer.astype(BF16)

    def mix(weights, blocks):
        blocks = jnp.concatenate(blocks, axis=1).astype(BF16)
        mixes = dot(weights.astype(BF16), blocks) * (1.0 / DEPTH)
        for h in range(OUTER_LATENT):
            mixed[pl.ds(h, KINDS, stride=32), :] = mixes[:, h * 128 : (h + 1) * 128]
        turned = jnp.concatenate([mixed[v * 32 : (v + 1) * 32] for v in range(KINDS)], axis=1)
        return halves_f32(turned)

    mixes = mix(
        acts[:, OUTER_LATENT : 2 * OUTER_LATENT],
        [w_out_v[h * 32 : (h + 1) * 32] for h in range(OUTER_LATENT)],
    ) + mix(
        acts[:, :OUTER_LATENT],
        [w_out_v[pl.ds(e, 32, stride=32), :] for e in range(OUTER_LATENT)],
    )
    fold[...] = jnp.transpose(jnp.concatenate(mixes, axis=0)).astype(BF16)

    def reduce(block, part, recv, ring, total, others):
        recv[slot] = part[block]
        wait_all(recv.at[pl.ds(0, PLANE - 1)], plane_recv)
        ring[z] = jnp.sum(recv[...].astype(F32), axis=0).astype(ring.dtype)
        for step in RING_STEPS:
            pltpu.make_async_remote_copy(
                src_ref=ring.at[z],
                dst_ref=ring.at[z],
                send_sem=ring_send,
                recv_sem=ring_recv,
                device_id=(dp, zs[step] + x_hi),
                device_id_type=MESH,
            ).start()
        wait_all(ring.at[pl.ds(0, RINGS - 1)], ring_recv)
        total[block] = jnp.sum(ring[...].astype(F32), axis=0).astype(total.dtype)
        for _, peer in peers:
            pltpu.make_async_remote_copy(
                src_ref=total.at[block],
                dst_ref=total.at[block],
                send_sem=all_send,
                recv_sem=all_recv.at[others],
                device_id=peer,
                device_id_type=MESH,
            ).start()

    @owns_pair
    def _():
        reduce(slot, pair_part, pair_recv, pair_ring, pair_total, 0)
        wait_all(pair_total.at[pl.ds(0, PAIR_BLOCKS - 1)], all_recv.at[0])
        wait_all(wide_total, all_recv.at[1])

    @owns_wide
    def _():
        reduce(slot - PAIR_BLOCKS, wide_part, wide_recv, wide_ring, wide_total, 1)
        wait_all(pair_total, all_recv.at[0])
        wait_all(wide_total.at[pl.ds(0, 1)], all_recv.at[1])

    @pl.when(slot >= BLOCKS)
    def _():
        wait_all(pair_total, all_recv.at[0])
        wait_all(wide_total, all_recv.at[1])

    summed = pair_total[...].reshape(KINDS * KINDS, 128)
    mixed[0 : KINDS * KINDS] = summed.astype(F32)
    by_first = jnp.concatenate([mixed[v * KINDS : (v + 1) * KINDS] for v in range(KINDS)], axis=1)
    by_second = jnp.concatenate(
        [mixed[pl.ds(u, KINDS, stride=KINDS), :] for u in range(KINDS)], axis=1
    )
    act = dot(jnp.concatenate([by_first, by_second], axis=0).astype(BF16), fold[...])
    act = jnp.where(low_lane, act[:KINDS], act[KINDS:])
    act = act + pltpu.roll(act, 96, 1)
    act = jnp.where(iota((1, 128), 1) < OUTER_LATENT, act, pltpu.roll(act, 96, 1))
    act = jnp.where((iota((KINDS, 128), 0) < SYMBOL_KINDS) & low_lane, act, 0.0)
    w_out_grad = dot(outer_v[...], summed)
    act_parts = jnp.concatenate(halves_f32(act), axis=0)
    act_parts = act_parts.astype(BF16)
    norm_grad = dot(act_parts, pair_turned[...])
    norm_grad = norm_grad[:KINDS] + norm_grad[KINDS:]
    wide[...] = dot(normed_twice[...], act_parts)
    w_pair_grad = wide[pl.ds(0, 128, stride=2), :] + pltpu.roll(
        wide[pl.ds(1, 128, stride=2), :], 64, 1
    )
    gained = norm_grad * gain
    feat = jnp.concatenate([wide_total[0][:KINDS], wide_total[1][:KINDS]], axis=1)
    table_grad = feat + inverse * (
        gained
        - jnp.mean(gained, axis=1, keepdims=True)
        - unit * jnp.mean(gained * unit, axis=1, keepdims=True)
    )
    gain_grad = jnp.sum(norm_grad * unit, axis=0, keepdims=True)
    shift_grad = jnp.sum(norm_grad, axis=0, keepdims=True)
    bias_grad = jnp.sum(act, axis=0, keepdims=True)

    shifted[0:8] = jnp.zeros((8, 128), F32)
    shifted[8:1032] = pltpu.roll(w_out_grad, 64, 1)
    shifted[1032:1088] = jnp.zeros((56, 128), F32)
    shifted[1032:1033] = pltpu.roll(wide_total[0][KINDS : KINDS + 1], 64, 1)
    shifted[pl.ds(1033, SYMBOL_KINDS, stride=2), :] = pltpu.roll(
        table_grad[:SYMBOL_KINDS, :128], 64, 1
    )
    shifted[pl.ds(1034, SYMBOL_KINDS, stride=2), :] = pltpu.roll(
        table_grad[:SYMBOL_KINDS, 128:], 64, 1
    )
    grad_ref[128:ROWS] = jnp.where(low_lane, shifted[3:1083], shifted[4:1084])
    grad_ref[0:4] = jnp.concatenate(
        [gain_grad[:, :128], gain_grad[:, 128:], shift_grad[:, :128], shift_grad[:, 128:]], axis=0
    )
    grad_ref[4:132] = w_pair_grad
    grad_ref[132:133] = jnp.where(low_lane, bias_grad, grad_ref[132:133])
    pair_sum = wide_total[0][KINDS : KINDS + 1]
    single = gain_grad * gain_grad + shift_grad * shift_grad
    single = single[:, :128] + single[:, 128:] + bias_grad * bias_grad + pair_sum * pair_sum
    by_kind = jnp.where(iota((KINDS, FEATURE_WIDTH), 0) < SYMBOL_KINDS, table_grad, 0.0)
    by_kind = jnp.sum((by_kind * by_kind).reshape(KINDS // 8, 8, FEATURE_WIDTH), axis=0)
    squares = (
        jnp.sum((w_out_grad * w_out_grad).reshape(128, 8, 128), axis=0)
        + jnp.sum((w_pair_grad * w_pair_grad).reshape(16, 8, 128), axis=0)
        + by_kind[:, :128]
        + by_kind[:, 128:]
        + wide_total[1][KINDS:]
        + jnp.where(iota((8, 128), 0) == 0, single, 0.0)
    )
    norm = jnp.sum(squares)
    norm = jnp.sqrt(jnp.full((1, 512), norm, F32))
    clip_ref[...] = jnp.minimum(1.0, clip_norm / (norm + 1e-06))

    wait_all(codes.at[pl.ds(0, CROP - 1)], code_send)

    def finish(recv, ring, pairs, wides):
        wait_all(pair_part.at[pl.ds(0, pairs)], plane_send.at[0])
        wait_all(wide_part.at[pl.ds(0, wides)], plane_send.at[1])
        if recv is not None:
            wait_all(ring.at[pl.ds(0, RINGS - 1)], ring_send)
            wait_all(recv.at[pl.ds(0, PLANE - 1)], all_send)

    @owns_pair
    def _():
        finish(pair_recv, pair_ring, PAIR_BLOCKS - 1, 2)

    @owns_wide
    def _():
        finish(wide_recv, wide_ring, PAIR_BLOCKS, 1)

    @pl.when(slot >= BLOCKS)
    def _():
        finish(None, None, PAIR_BLOCKS, 2)


def in_hbm(array):
    return pltpu.with_memory_space_constraint(array, pltpu.HBM)


def gradients(*arrays):
    return pl.pallas_call(
        kernel,
        out_shape=(
            jax.ShapeDtypeStruct((ROWS, 128), F32),
            jax.ShapeDtypeStruct((1, 512), F32),
        ),
        in_specs=[pl.BlockSpec(memory_space=pltpu.HBM)] * 6,
        out_specs=(
            pl.BlockSpec(memory_space=pltpu.VMEM),
            pl.BlockSpec(memory_space=pltpu.VMEM),
        ),
        scratch_shapes=[
            pltpu.VMEM((RES, DEPTH), jnp.int32),
            pltpu.VMEM((RES, DEPTH), jnp.int32),
            pltpu.VMEM((RES, 128, 128), BF16),
            pltpu.VMEM((RES, 64, 128), BF16),
            pltpu.VMEM((RES, 64, 128), BF16),
            pltpu.VMEM((DEPTH * RES, FEATURE_WIDTH), BF16),
            pltpu.VMEM((PARAMS,), F32),
            pltpu.VMEM((256, 512), F32),
            pltpu.VMEM((CROP, RES, DEPTH), BF16),
            pltpu.VMEM((KINDS * KINDS, RES * 128), BF16),
            pltpu.VMEM((KINDS * KINDS, RES * 64), BF16),
            pltpu.VMEM((KINDS * KINDS, RES * 64), BF16),
            pltpu.VMEM((PAIR_BLOCKS, PAIR_ROWS, 128), BF16),
            pltpu.VMEM((PLANE, PAIR_ROWS, 128), BF16),
            pltpu.VMEM((RINGS, PAIR_ROWS, 128), BF16),
            pltpu.VMEM((PAIR_BLOCKS, PAIR_ROWS, 128), BF16),
            pltpu.VMEM((2, WIDE_ROWS, 128), F32),
            pltpu.VMEM((PLANE, WIDE_ROWS, 128), F32),
            pltpu.VMEM((RINGS, WIDE_ROWS, 128), F32),
            pltpu.VMEM((2, WIDE_ROWS, 128), F32),
            pltpu.VMEM((1024, KINDS * KINDS), BF16),
            pltpu.VMEM((KINDS * 128, 128), BF16),
            pltpu.VMEM((ROWS + 8, 128), F32),
            pltpu.VMEM((FEATURE_WIDTH, 128), F32),
            pltpu.VMEM((1024, 128), F32),
            pltpu.VMEM((KINDS * 32, 128), F32),
            pltpu.VMEM((FEATURE_WIDTH, 128), F32),
            pltpu.VMEM((128, FEATURE_WIDTH), BF16),
            pltpu.VMEM((FEATURE_WIDTH, 2 * KINDS), BF16),
            pltpu.SemaphoreType.DMA((5,)),
            pltpu.SemaphoreType.DMA((CROP,)),
            pltpu.SemaphoreType.DMA,
            pltpu.SemaphoreType.DMA((len(STAGES),)),
            pltpu.SemaphoreType.DMA((2,)),
            pltpu.SemaphoreType.DMA,
            pltpu.SemaphoreType.DMA,
            pltpu.SemaphoreType.DMA,
            pltpu.SemaphoreType.DMA,
            pltpu.SemaphoreType.DMA((2,)),
        ],
        compiler_params=pltpu.CompilerParams(
            collective_id=0, has_side_effects=True, vmem_limit_bytes=40 * 1024 * 1024
        ),
        cost_estimate=pl.CostEstimate(
            flops=3_000_000_000, bytes_accessed=40_000_000, transcendentals=0
        ),
    )(*[in_hbm(array) for array in arrays])


def adam_update(master, moment_one, moment_two, scaled):
    first = beta_first * moment_one + (1.0 - beta_first) * scaled
    second = beta_second * moment_two + (1.0 - beta_second) * scaled * scaled
    fix_first = 1.0 - beta_first**STEP
    fix_second = 1.0 - beta_second**STEP
    update = first * (learn_rate / fix_first) / (jnp.sqrt(second * (1.0 / fix_second)) + adam_eps)
    return (master - update, first, second)


def update_kernel(
    grad_ref,
    clip_ref,
    master_ref,
    one_ref,
    two_ref,
    rest_grad_ref,
    rest_master_ref,
    rest_one_ref,
    rest_two_ref,
    *refs,
):
    outs, held, sems = refs[:8], refs[8:16], refs[16]
    clip = clip_ref[...]
    rest_step = rest_grad_ref.shape[0] // CHUNKS
    flat_step = 1024 * 19
    copies = []

    def send(n, where):
        copy = pltpu.make_async_copy(held[n].at[where], outs[n].at[where], sems.at[len(copies)])
        copy.start()
        copies.append(copy)

    for chunk in range(CHUNKS):
        where = pl.ds(chunk * rest_step, rest_step)
        new = adam_update(
            rest_master_ref[where], rest_one_ref[where], rest_two_ref[where], rest_grad_ref[where] * clip
        )
        for n, value in enumerate(new + (new[0],)):
            held[4 + n][where] = value.astype(held[4 + n].dtype)
            send(4 + n, where)
    factor = jnp.max(clip)
    for chunk in range(CHUNKS):
        start = chunk * flat_step
        where = pl.ds(start, min(flat_step, PARAMS - start))
        new = adam_update(master_ref[where], one_ref[where], two_ref[where], grad_ref[where] * factor)
        for n, value in enumerate(new + (new[0],)):
            held[n][where] = value.astype(held[n].dtype)
            send(n, where)
    for copy in copies:
        copy.wait()


def updates(grad, clip, master, one, two, rest_grad, rest_master, rest_one, rest_two):
    flat = [jax.ShapeDtypeStruct(master.shape, dtype) for dtype in (F32, F32, F32, BF16)]
    rows = [jax.ShapeDtypeStruct(rest_master.shape, dtype) for dtype in (F32, F32, F32, BF16)]
    return pl.pallas_call(
        update_kernel,
        out_shape=tuple(flat + rows),
        in_specs=[pl.BlockSpec(memory_space=pltpu.VMEM)] * 9,
        out_specs=tuple([pl.BlockSpec(memory_space=pltpu.HBM)] * 8),
        scratch_shapes=[pltpu.VMEM(out.shape, out.dtype) for out in flat + rows]
        + [pltpu.SemaphoreType.DMA((8 * CHUNKS,))],
        compiler_params=pltpu.CompilerParams(vmem_limit_bytes=20 * 1024 * 1024),
        cost_estimate=pl.CostEstimate(
            flops=5_000_000, bytes_accessed=8_000_000, transcendentals=0
        ),
    )(grad, clip, master, one, two, rest_grad, rest_master, rest_one, rest_two)


def shards(
    symbol_codes,
    aligned_validity,
    pair_update_cotangent,
    aligned_feature_adjoint,
    local_master_weights,
    local_first_moment,
    local_second_moment,
    remaining_master_weights,
    remaining_first_moment,
    remaining_second_moment,
    remaining_gradient,
):
    gradient, clip = gradients(
        jnp.transpose(symbol_codes[0]),
        jnp.transpose(aligned_validity[0]),
        pair_update_cotangent.reshape(RES, CROP, RES, 128),
        aligned_feature_adjoint.reshape(DEPTH * RES, FEATURE_WIDTH),
        local_master_weights,
        remaining_gradient,
    )
    return updates(
        gradient.reshape(-1),
        clip,
        local_master_weights,
        local_first_moment,
        local_second_moment,
        remaining_gradient,
        remaining_master_weights,
        remaining_first_moment,
        remaining_second_moment,
    )


def solution(mesh):
    return jax.shard_map(
        shards,
        mesh=mesh,
        in_specs=(
            P("dp", None, "dap"),
            P("dp", None, "dap"),
            P("dp", "dap", None, None),
            P("dp", None, "dap", None),
            P(),
            P(),
            P(),
            P(("dp", "dap"), None),
            P(("dp", "dap"), None),
            P(("dp", "dap"), None),
            P(("dp", "dap"), None),
        ),
        out_specs=(
            P(),
            P(),
            P(),
            P(),
            P(("dp", "dap"), None),
            P(("dp", "dap"), None),
            P(("dp", "dap"), None),
            P(("dp", "dap"), None),
        ),
        check_vma=False,
    )
```

```python
import jax
import jax.numpy as jnp
from jax import lax
from jax.experimental import pallas as pl
from jax.experimental.pallas import tpu as pltpu
from jax.sharding import PartitionSpec as P

FEATURE_WIDTH = 256
OUTER_LATENT = 32
SYMBOL_KINDS = 23
STEP = 10
PARAMS = 154048
ROWS = 1208
KINDS = 24
MASKED = 24.0
DEPTH = 128
RES = 16
LENGTH = 256
PLANE = 32
RINGS = 8
CROP = 16

PAIR_ROWS = 2 * KINDS
PAIR_BLOCKS = KINDS // 2
WIDE_ROWS = 32
BLOCKS = PAIR_BLOCKS + 2
CHUNKS = 8

beta_first = 0.9
beta_second = 0.999
adam_eps = 1e-06
learn_rate = 0.001
clip_norm = 0.1
norm_eps = 1e-05
ROOT_FLOOR = 1e-36

MESH = pl.DeviceIdType.MESH
F32 = jnp.float32
BF16 = jnp.bfloat16
F8 = jnp.float8_e4m3fn


def ring_hops(step, size):
    return min(step, size - step)


PLANE_STEPS = sorted(
    (-ring_hops(dx, 4) - ring_hops(dy, 4), dx, dy, dc)
    for dx in range(4)
    for dy in range(4)
    for dc in range(2)
    if dx + dy + dc > 0
)
RING_STEPS = sorted(range(1, RINGS), key=lambda s: -ring_hops(s, RINGS))
CROP_STEPS = sorted(
    (-ring_hops(dz, RINGS) - 2 * dx, dx, dz)
    for dz in range(RINGS)
    for dx in range(2)
    if dz + dx > 0
)
STAGES = ((0, 8), (8, 12), (12, 16))


def iota(shape, axis):
    return lax.broadcasted_iota(jnp.int32, shape, axis)


def dot(a, b):
    return jnp.dot(a, b, preferred_element_type=F32)


def dot_nt(a, b):
    return lax.dot_general(a, b, (((1,), (1,)), ((), ())), preferred_element_type=F32)


def dot_tn(a, b):
    return lax.dot_general(a, b, (((0,), (0,)), ((), ())), preferred_element_type=F32)


def halves_f32(x):
    high = x.astype(BF16).astype(F32)
    return high, x - high


def kernel(
    tok_hbm,
    valid_hbm,
    pair_hbm,
    adj_hbm,
    w_hbm,
    rest_hbm,
    grad_ref,
    clip_ref,
    tok_v,
    valid_v,
    pair_near,
    pair_middle,
    pair_far,
    adj_v,
    w_v,
    rest_v,
    codes,
    counts_near,
    counts_middle,
    counts_far,
    pair_part,
    pair_recv,
    pair_ring,
    pair_total,
    wide_part,
    wide_recv,
    wide_ring,
    wide_total,
    outer_v,
    fold,
    shifted,
    wide,
    w_out_v,
    mixed,
    pair_rows,
    pair_turned,
    normed_twice,
    local_sem,
    block_sem,
    code_send,
    code_recv,
    plane_send,
    plane_recv,
    ring_send,
    ring_recv,
    all_send,
    all_recv,
):
    dp = lax.axis_index("dp")
    dap = lax.axis_index("dap")
    z = lax.div(dap, 2)
    x_hi = lax.rem(dap, 2)
    core = lax.rem(dp, 2)
    y = lax.rem(lax.div(dp, 2), 4)
    x = x_hi * 2 + lax.div(dp, 8)

    xs = [lax.rem(x + dx, 4) for dx in range(4)]
    xs = [(lax.rem(value, 2) * 8, lax.div(value, 2)) for value in xs]
    ys = [lax.rem(y + dy, 4) * 2 for dy in range(4)]
    cores = [lax.rem(core + dc, 2) for dc in range(2)]

    def in_plane(dx, dy, dc):
        low, high = xs[dx]
        return cores[dc] * 16 + low + ys[dy] + high, (low + ys[dy] + cores[dc], z * 2 + high)

    slot = in_plane(0, 0, 0)[0]
    peers = [in_plane(*step[1:]) for step in PLANE_STEPS]
    zs = [lax.rem(z + dz, RINGS) * 2 for dz in range(RINGS)]
    mates = [zs[dz] + (1 - x_hi if dx else x_hi) for _, dx, dz in CROP_STEPS]
    order = [dap] + mates[::-1]

    barrier = pltpu.get_barrier_semaphore()
    greetings = [(step[0], (dp, mate)) for step, mate in zip(CROP_STEPS, mates)]
    greetings += [(step[0], peer) for step, (_, peer) in zip(PLANE_STEPS, peers)]
    greetings = [device for _, device in sorted(greetings, key=lambda pair: pair[0])]
    for device in greetings:
        pl.semaphore_signal(barrier, inc=1, device_id=device, device_id_type=MESH)


    loads = []
    for n, (src, dst) in enumerate(
        (
            (tok_hbm, tok_v),
            (valid_hbm, valid_v),
            (w_hbm, w_v),
            (adj_hbm, adj_v),
            (rest_hbm, rest_v),
        )
    ):
        copy = pltpu.make_async_copy(src, dst, local_sem.at[n])
        copy.start()
        loads.append(copy)

    cotangents = (pair_near, pair_middle, pair_far)
    for stage, (start, stop) in enumerate(STAGES):
        for n in range(start, stop):
            copy = pltpu.make_async_copy(
                pair_hbm.at[:, order[n]],
                cotangents[stage].at[:, pl.ds((n - start) * RES, RES)],
                block_sem.at[n],
            )
            copy.start()
            loads.append(copy)

    loads[0].wait()
    loads[1].wait()
    tok = tok_v[...].astype(F32)
    own = jnp.where(valid_v[...] != 0, tok, MASKED)
    codes[dap] = own.astype(BF16)
    pl.semaphore_wait(barrier, CROP - 1 + PLANE - 1)

    def wait_all(ref, sem):
        pltpu.make_async_copy(ref, ref, sem).wait()

    for n in range(CROP - 1, 0, -1):
        pltpu.make_async_remote_copy(
            src_ref=codes.at[dap],
            dst_ref=codes.at[dap],
            send_sem=code_send,
            recv_sem=code_recv.at[[start <= n < stop for start, stop in STAGES].index(True)],
            device_id=(dp, order[n]),
            device_id_type=MESH,
        ).start()

    spread = (iota((RES, 128), 1) % RES == iota((RES, 128), 0)).astype(F32)
    tiled = dot_tn(tok, spread)
    tiled = jnp.where(iota((DEPTH, 128), 0) % 8 == iota((DEPTH, 128), 1) // RES, tiled, 0.0)
    gather = (iota((RES, DEPTH), 1) // 8 == iota((RES, DEPTH), 0)).astype(F32)
    flat = dot(gather, tiled)
    kind = iota((KINDS, 128), 0).astype(F32)
    hot = jnp.concatenate(
        [(flat[q : q + 1, :] == kind).astype(F32) for q in range(RES)], axis=1
    ).astype(BF16)
    loads[3].wait()
    feat = dot(hot, adj_v[...])
    loads[4].wait()
    rest = rest_v[...]
    square = jnp.sum((rest * rest).reshape(32, 8, 512), axis=0)
    square = square[:, :128] + square[:, 128:256] + square[:, 256:384] + square[:, 384:]
    for copy in loads[5:]:
        copy.wait()
    pair_sum = jnp.zeros((16, 128), F32)
    for cotangent in cotangents:
        rows = cotangent.shape[0] * cotangent.shape[1]
        pair_sum = pair_sum + dot(jnp.ones((16, rows), BF16), cotangent[...].reshape(rows, 128))
    wide_part[0] = jnp.concatenate([feat[:, :128], pair_sum[:8]], axis=0)
    wide_part[1] = jnp.concatenate([feat[:, 128:], square], axis=0)

    def owner_of(p):
        return ((p % 16 // 2) * 2 + p // 16, z * 2 + p % 2)

    def plane_copy(part, recv, block, target):
        return pltpu.make_async_remote_copy(
            src_ref=part.at[block],
            dst_ref=recv.at[slot],
            send_sem=plane_send.at[0 if part is pair_part else 1],
            recv_sem=plane_recv,
            device_id=owner_of(target),
            device_id_type=MESH,
        )

    def to_owners(part, recv, first):
        for block in range(part.shape[0]):

            @pl.when(slot != first + block)
            def _():
                plane_copy(part, recv, block, first + block).start()

    def owns_pair(then):
        pl.when(slot < PAIR_BLOCKS)(then)

    def owns_wide(then):
        pl.when((slot >= PAIR_BLOCKS) & (slot < BLOCKS))(then)

    to_owners(wide_part, wide_recv, PAIR_BLOCKS)

    low_lane = iota((1, 128), 1) < 64
    hot_own = jnp.concatenate(
        [(own[i : i + 1, :] == kind).astype(F32) for i in range(RES)], axis=0
    ).astype(F8)

    sums = jnp.zeros((KINDS * KINDS, 128), F32)
    for stage, (start, stop) in enumerate(STAGES):
        wait_all(codes.at[pl.ds(0, stop - max(start, 1))], code_recv.at[stage])
        every = jnp.concatenate([codes[block].astype(F32) for block in order[start:stop]], axis=0)
        every = jnp.transpose(every)
        size = (stop - start) * RES
        counts = (counts_near, counts_middle, counts_far)[stage]
        count = 256 // size
        for first in range(0, KINDS, count):
            hot_all = jnp.concatenate(
                [(every == float(v)).astype(F32) for v in range(first, first + count)], axis=1
            )
            all_pairs = dot(hot_own, hot_all.astype(F8))
            for p in range(first // 2, (first + count) // 2):
                if size == 128:
                    both = all_pairs.reshape(RES, KINDS, 256)
                    both = jnp.concatenate([both[:, :, :128], both[:, :, 128:]], axis=1)
                else:
                    start_lane = (p - first // 2) * 128
                    both = all_pairs[:, start_lane : start_lane + 128]
                    turned = pltpu.roll(both, 64, 1).reshape(RES // 2, 2, KINDS, 128)
                    both = both.reshape(RES // 2, 2, KINDS, 128)
                    both = jnp.concatenate(
                        [
                            jnp.where(low_lane, both[:, 0], turned[:, 1]),
                            jnp.where(low_lane, turned[:, 0], both[:, 1]),
                        ],
                        axis=1,
                    )
                both = both.astype(BF16)
                for i in range(both.shape[0]):
                    counts[p * PAIR_ROWS : (p + 1) * PAIR_ROWS, i * 128 : (i + 1) * 128] = both[i]
        sums = sums + dot(counts[...], cotangents[stage][...].reshape(RES * size, 128))
    pair_part[...] = sums.astype(BF16).reshape(PAIR_BLOCKS, PAIR_ROWS, 128)
    to_owners(pair_part, pair_recv, 0)

    loads[2].wait()
    weights = jnp.concatenate(
        [
            w_v[pl.ds(0, 153600)].reshape(1200, 128),
            jnp.concatenate(
                [w_v[pl.ds(153600, PARAMS - 153600)], jnp.zeros((ROWS * 128 - PARAMS,), F32)]
            ).reshape(8, 128),
        ],
        axis=0,
    )
    weights = weights.astype(BF16).astype(F32)
    shifted[0:ROWS] = pltpu.roll(weights, 64, 1)
    w_out_v[...] = jnp.where(
        low_lane, shifted[pl.ds(132, 1024), :], shifted[pl.ds(133, 1024), :]
    )
    first = jnp.where(
        low_lane,
        shifted[pl.ds(1157, KINDS, stride=2), :],
        shifted[pl.ds(1158, KINDS, stride=2), :],
    )
    second = jnp.where(
        low_lane,
        shifted[pl.ds(1158, KINDS, stride=2), :],
        shifted[pl.ds(1159, KINDS, stride=2), :],
    )
    table = jnp.concatenate([first, second], axis=1)
    table = jnp.where(iota((KINDS, FEATURE_WIDTH), 0) < SYMBOL_KINDS, table, 0.0)
    center = jnp.mean(table, axis=1, keepdims=True)
    variance = jnp.mean((table - center) ** 2, axis=1, keepdims=True)
    inverse = lax.rsqrt(variance + norm_eps)
    unit = (table - center) * inverse
    gain = jnp.concatenate([weights[0:1], weights[1:2]], axis=1)
    shift = jnp.concatenate([weights[2:3], weights[3:4]], axis=1)
    normed = (unit * gain + shift).astype(BF16).astype(F32)
    w_rows = weights[4:132]
    pair_rows[pl.ds(0, 128, stride=2), :] = jnp.where(low_lane, w_rows, 0.0)
    pair_rows[pl.ds(1, 128, stride=2), :] = jnp.where(low_lane, pltpu.roll(w_rows, 64, 1), 0.0)
    w_pair = pair_rows[...]
    pair_turned[...] = jnp.transpose(w_pair).astype(BF16)
    bias = jnp.where(low_lane, weights[132:133], 0.0)
    acts = (dot(normed, w_pair) + bias).astype(BF16).astype(F32)
    acts = jnp.where(iota((KINDS, 128), 0) < SYMBOL_KINDS, acts, 0.0)

    normed_twice[...] = jnp.transpose(jnp.concatenate([normed, normed], axis=0)).astype(BF16)

    he_row = iota((1024, 128), 0)
    lane = iota((1024, 128), 1)
    acts_t = jnp.transpose(acts).astype(BF16)
    left_of = dot((he_row // 32 == lane).astype(F32).astype(BF16), acts_t).astype(BF16)
    right_of = dot((he_row % 32 == lane - 32).astype(F32).astype(BF16), acts_t).astype(BF16)
    uv = iota((KINDS, KINDS * KINDS), 1)
    kind_row = iota((KINDS, KINDS * KINDS), 0)
    outer = dot(left_of, (uv % KINDS == kind_row).astype(F32).astype(BF16)) * (1.0 / DEPTH)
    outer = outer * dot(right_of, (uv // KINDS == kind_row).astype(F32).astype(BF16))
    outer_v[...] = outer.astype(BF16)

    def mix(weights, blocks):
        blocks = jnp.concatenate(blocks, axis=1).astype(BF16)
        mixes = dot(weights.astype(BF16), blocks) * (1.0 / DEPTH)
        for h in range(OUTER_LATENT):
            mixed[pl.ds(h, KINDS, stride=32), :] = mixes[:, h * 128 : (h + 1) * 128]
        turned = jnp.concatenate([mixed[v * 32 : (v + 1) * 32] for v in range(KINDS)], axis=1)
        return halves_f32(turned)

    mixes = mix(
        acts[:, OUTER_LATENT : 2 * OUTER_LATENT],
        [w_out_v[h * 32 : (h + 1) * 32] for h in range(OUTER_LATENT)],
    ) + mix(
        acts[:, :OUTER_LATENT],
        [w_out_v[pl.ds(e, 32, stride=32), :] for e in range(OUTER_LATENT)],
    )
    fold[...] = jnp.transpose(jnp.concatenate(mixes, axis=0)).astype(BF16)

    def reduce(block, part, recv, ring, total, others):
        recv[slot] = part[block]
        wait_all(recv.at[pl.ds(0, PLANE - 1)], plane_recv)
        ring[z] = jnp.sum(recv[...].astype(F32), axis=0).astype(ring.dtype)
        for step in RING_STEPS:
            pltpu.make_async_remote_copy(
                src_ref=ring.at[z],
                dst_ref=ring.at[z],
                send_sem=ring_send,
                recv_sem=ring_recv,
                device_id=(dp, zs[step] + x_hi),
                device_id_type=MESH,
            ).start()
        wait_all(ring.at[pl.ds(0, RINGS - 1)], ring_recv)
        total[block] = jnp.sum(ring[...].astype(F32), axis=0).astype(total.dtype)
        for _, peer in peers:
            pltpu.make_async_remote_copy(
                src_ref=total.at[block],
                dst_ref=total.at[block],
                send_sem=all_send,
                recv_sem=all_recv.at[others],
                device_id=peer,
                device_id_type=MESH,
            ).start()

    @owns_pair
    def _():
        reduce(slot, pair_part, pair_recv, pair_ring, pair_total, 0)
        wait_all(pair_total.at[pl.ds(0, PAIR_BLOCKS - 1)], all_recv.at[0])
        wait_all(wide_total, all_recv.at[1])

    @owns_wide
    def _():
        reduce(slot - PAIR_BLOCKS, wide_part, wide_recv, wide_ring, wide_total, 1)
        wait_all(pair_total, all_recv.at[0])
        wait_all(wide_total.at[pl.ds(0, 1)], all_recv.at[1])

    @pl.when(slot >= BLOCKS)
    def _():
        wait_all(pair_total, all_recv.at[0])
        wait_all(wide_total, all_recv.at[1])

    summed = pair_total[...].reshape(KINDS * KINDS, 128)
    mixed[0 : KINDS * KINDS] = summed.astype(F32)
    by_first = jnp.concatenate([mixed[v * KINDS : (v + 1) * KINDS] for v in range(KINDS)], axis=1)
    by_second = jnp.concatenate(
        [mixed[pl.ds(u, KINDS, stride=KINDS), :] for u in range(KINDS)], axis=1
    )
    act = dot(jnp.concatenate([by_first, by_second], axis=0).astype(BF16), fold[...])
    act = jnp.where(low_lane, act[:KINDS], act[KINDS:])
    act = act + pltpu.roll(act, 96, 1)
    act = jnp.where(iota((1, 128), 1) < OUTER_LATENT, act, pltpu.roll(act, 96, 1))
    act = jnp.where((iota((KINDS, 128), 0) < SYMBOL_KINDS) & low_lane, act, 0.0)
    w_out_grad = dot(outer_v[...], pltpu.roll(mixed[0 : KINDS * KINDS], 64, 1).astype(BF16))
    act_parts = jnp.concatenate(halves_f32(act), axis=0)
    act_parts = act_parts.astype(BF16)
    norm_grad = dot(act_parts, pair_turned[...])
    norm_grad = norm_grad[:KINDS] + norm_grad[KINDS:]
    wide[...] = dot(normed_twice[...], act_parts)
    w_pair_grad = wide[pl.ds(0, 128, stride=2), :] + pltpu.roll(
        wide[pl.ds(1, 128, stride=2), :], 64, 1
    )
    gained = norm_grad * gain
    feat = jnp.concatenate([wide_total[0][:KINDS], wide_total[1][:KINDS]], axis=1)
    table_grad = feat + inverse * (
        gained
        - jnp.mean(gained, axis=1, keepdims=True)
        - unit * jnp.mean(gained * unit, axis=1, keepdims=True)
    )
    gain_grad = jnp.sum(norm_grad * unit, axis=0, keepdims=True)
    shift_grad = jnp.sum(norm_grad, axis=0, keepdims=True)
    bias_grad = jnp.sum(act, axis=0, keepdims=True)

    shifted[0:8] = jnp.zeros((8, 128), F32)
    shifted[8:1032] = w_out_grad
    shifted[1032:1088] = jnp.zeros((56, 128), F32)
    shifted[1032:1033] = pltpu.roll(wide_total[0][KINDS : KINDS + 1], 64, 1)
    shifted[pl.ds(1033, SYMBOL_KINDS, stride=2), :] = pltpu.roll(
        table_grad[:SYMBOL_KINDS, :128], 64, 1
    )
    shifted[pl.ds(1034, SYMBOL_KINDS, stride=2), :] = pltpu.roll(
        table_grad[:SYMBOL_KINDS, 128:], 64, 1
    )
    grad_ref[128:ROWS] = jnp.where(low_lane, shifted[3:1083], shifted[4:1084])
    grad_ref[0:4] = jnp.concatenate(
        [gain_grad[:, :128], gain_grad[:, 128:], shift_grad[:, :128], shift_grad[:, 128:]], axis=0
    )
    grad_ref[4:132] = w_pair_grad
    grad_ref[132:133] = jnp.where(low_lane, bias_grad, grad_ref[132:133])
    pair_sum = wide_total[0][KINDS : KINDS + 1]
    single = gain_grad * gain_grad + shift_grad * shift_grad
    single = single[:, :128] + single[:, 128:] + bias_grad * bias_grad + pair_sum * pair_sum
    by_kind = jnp.where(iota((KINDS, FEATURE_WIDTH), 0) < SYMBOL_KINDS, table_grad, 0.0)
    by_kind = jnp.sum((by_kind * by_kind).reshape(KINDS // 8, 8, FEATURE_WIDTH), axis=0)
    squares = (
        jnp.sum((w_out_grad * w_out_grad).reshape(128, 8, 128), axis=0)
        + jnp.sum((w_pair_grad * w_pair_grad).reshape(16, 8, 128), axis=0)
        + by_kind[:, :128]
        + by_kind[:, 128:]
        + wide_total[1][KINDS:]
        + jnp.where(iota((8, 128), 0) == 0, single, 0.0)
    )
    norm = jnp.sum(squares)
    norm = jnp.sqrt(jnp.full((1, 512), norm, F32))
    clip_ref[...] = jnp.minimum(1.0, clip_norm / (norm + 1e-06))

    wait_all(codes.at[pl.ds(0, CROP - 1)], code_send)

    def finish(recv, ring, pairs, wides):
        wait_all(pair_part.at[pl.ds(0, pairs)], plane_send.at[0])
        wait_all(wide_part.at[pl.ds(0, wides)], plane_send.at[1])
        if recv is not None:
            wait_all(ring.at[pl.ds(0, RINGS - 1)], ring_send)
            wait_all(recv.at[pl.ds(0, PLANE - 1)], all_send)

    @owns_pair
    def _():
        finish(pair_recv, pair_ring, PAIR_BLOCKS - 1, 2)

    @owns_wide
    def _():
        finish(wide_recv, wide_ring, PAIR_BLOCKS, 1)

    @pl.when(slot >= BLOCKS)
    def _():
        finish(None, None, PAIR_BLOCKS, 2)


def in_hbm(array):
    return pltpu.with_memory_space_constraint(array, pltpu.HBM)


def gradients(*arrays):
    return pl.pallas_call(
        kernel,
        out_shape=(
            jax.ShapeDtypeStruct((ROWS, 128), F32),
            jax.ShapeDtypeStruct((1, 512), F32),
        ),
        in_specs=[pl.BlockSpec(memory_space=pltpu.HBM)] * 6,
        out_specs=(
            pl.BlockSpec(memory_space=pltpu.VMEM),
            pl.BlockSpec(memory_space=pltpu.VMEM),
        ),
        scratch_shapes=[
            pltpu.VMEM((RES, DEPTH), jnp.int32),
            pltpu.VMEM((RES, DEPTH), jnp.int32),
            pltpu.VMEM((RES, 128, 128), BF16),
            pltpu.VMEM((RES, 64, 128), BF16),
            pltpu.VMEM((RES, 64, 128), BF16),
            pltpu.VMEM((DEPTH * RES, FEATURE_WIDTH), BF16),
            pltpu.VMEM((PARAMS,), F32),
            pltpu.VMEM((256, 512), F32),
            pltpu.VMEM((CROP, RES, DEPTH), BF16),
            pltpu.VMEM((KINDS * KINDS, RES * 128), BF16),
            pltpu.VMEM((KINDS * KINDS, RES * 64), BF16),
            pltpu.VMEM((KINDS * KINDS, RES * 64), BF16),
            pltpu.VMEM((PAIR_BLOCKS, PAIR_ROWS, 128), BF16),
            pltpu.VMEM((PLANE, PAIR_ROWS, 128), BF16),
            pltpu.VMEM((RINGS, PAIR_ROWS, 128), BF16),
            pltpu.VMEM((PAIR_BLOCKS, PAIR_ROWS, 128), BF16),
            pltpu.VMEM((2, WIDE_ROWS, 128), F32),
            pltpu.VMEM((PLANE, WIDE_ROWS, 128), F32),
            pltpu.VMEM((RINGS, WIDE_ROWS, 128), F32),
            pltpu.VMEM((2, WIDE_ROWS, 128), F32),
            pltpu.VMEM((1024, KINDS * KINDS), BF16),
            pltpu.VMEM((KINDS * 128, 128), BF16),
            pltpu.VMEM((ROWS + 8, 128), F32),
            pltpu.VMEM((FEATURE_WIDTH, 128), F32),
            pltpu.VMEM((1024, 128), F32),
            pltpu.VMEM((KINDS * 32, 128), F32),
            pltpu.VMEM((FEATURE_WIDTH, 128), F32),
            pltpu.VMEM((128, FEATURE_WIDTH), BF16),
            pltpu.VMEM((FEATURE_WIDTH, 2 * KINDS), BF16),
            pltpu.SemaphoreType.DMA((5,)),
            pltpu.SemaphoreType.DMA((CROP,)),
            pltpu.SemaphoreType.DMA,
            pltpu.SemaphoreType.DMA((len(STAGES),)),
            pltpu.SemaphoreType.DMA((2,)),
            pltpu.SemaphoreType.DMA,
            pltpu.SemaphoreType.DMA,
            pltpu.SemaphoreType.DMA,
            pltpu.SemaphoreType.DMA,
            pltpu.SemaphoreType.DMA((2,)),
        ],
        compiler_params=pltpu.CompilerParams(
            collective_id=0, has_side_effects=True, vmem_limit_bytes=40 * 1024 * 1024
        ),
        cost_estimate=pl.CostEstimate(
            flops=3_000_000_000, bytes_accessed=40_000_000, transcendentals=0
        ),
    )(*[in_hbm(array) for array in arrays])


def adam_update(master, moment_one, moment_two, scaled):
    first = beta_first * moment_one + (1.0 - beta_first) * scaled
    second = beta_second * moment_two + (1.0 - beta_second) * scaled * scaled
    fix_first = 1.0 - beta_first**STEP
    fix_second = 1.0 - beta_second**STEP
    root = second * lax.rsqrt(jnp.maximum(second, ROOT_FLOOR)) * fix_second**-0.5
    size = root + adam_eps
    guess = pl.reciprocal(size, approx=True)
    guess = guess * (2.0 - size * guess)
    return (master - first * (learn_rate / fix_first) * guess, first, second)


def update_kernel(
    grad_ref,
    clip_ref,
    master_ref,
    one_ref,
    two_ref,
    rest_grad_ref,
    rest_master_ref,
    rest_one_ref,
    rest_two_ref,
    *refs,
):
    outs, held, sems = refs[:8], refs[8:16], refs[16]
    clip = clip_ref[...]
    rest_step = rest_grad_ref.shape[0] // CHUNKS
    flat_step = 1024 * 19
    copies = []

    def send(n, where):
        copy = pltpu.make_async_copy(held[n].at[where], outs[n].at[where], sems.at[len(copies)])
        copy.start()
        copies.append(copy)

    for chunk in range(CHUNKS):
        where = pl.ds(chunk * rest_step, rest_step)
        new = adam_update(
            rest_master_ref[where], rest_one_ref[where], rest_two_ref[where], rest_grad_ref[where] * clip
        )
        for n, value in enumerate(new + (new[0],)):
            held[4 + n][where] = value.astype(held[4 + n].dtype)
            send(4 + n, where)
    factor = jnp.max(clip)
    for chunk in range(CHUNKS):
        start = chunk * flat_step
        where = pl.ds(start, min(flat_step, PARAMS - start))
        new = adam_update(master_ref[where], one_ref[where], two_ref[where], grad_ref[where] * factor)
        for n, value in enumerate(new + (new[0],)):
            held[n][where] = value.astype(held[n].dtype)
            send(n, where)
    for copy in copies:
        copy.wait()


def updates(grad, clip, master, one, two, rest_grad, rest_master, rest_one, rest_two):
    flat = [jax.ShapeDtypeStruct(master.shape, dtype) for dtype in (F32, F32, F32, BF16)]
    rows = [jax.ShapeDtypeStruct(rest_master.shape, dtype) for dtype in (F32, F32, F32, BF16)]
    return pl.pallas_call(
        update_kernel,
        out_shape=tuple(flat + rows),
        in_specs=[pl.BlockSpec(memory_space=pltpu.VMEM)] * 9,
        out_specs=tuple([pl.BlockSpec(memory_space=pltpu.HBM)] * 8),
        scratch_shapes=[pltpu.VMEM(out.shape, out.dtype) for out in flat + rows]
        + [pltpu.SemaphoreType.DMA((8 * CHUNKS,))],
        compiler_params=pltpu.CompilerParams(vmem_limit_bytes=20 * 1024 * 1024),
        cost_estimate=pl.CostEstimate(
            flops=5_000_000, bytes_accessed=8_000_000, transcendentals=0
        ),
    )(grad, clip, master, one, two, rest_grad, rest_master, rest_one, rest_two)


def shards(
    symbol_codes,
    aligned_validity,
    pair_update_cotangent,
    aligned_feature_adjoint,
    local_master_weights,
    local_first_moment,
    local_second_moment,
    remaining_master_weights,
    remaining_first_moment,
    remaining_second_moment,
    remaining_gradient,
):
    gradient, clip = gradients(
        jnp.transpose(symbol_codes[0]),
        jnp.transpose(aligned_validity[0]),
        pair_update_cotangent.reshape(RES, CROP, RES, 128),
        aligned_feature_adjoint.reshape(DEPTH * RES, FEATURE_WIDTH),
        local_master_weights,
        remaining_gradient,
    )
    return updates(
        gradient.reshape(-1),
        clip,
        local_master_weights,
        local_first_moment,
        local_second_moment,
        remaining_gradient,
        remaining_master_weights,
        remaining_first_moment,
        remaining_second_moment,
    )


def solution(mesh):
    return jax.shard_map(
        shards,
        mesh=mesh,
        in_specs=(
            P("dp", None, "dap"),
            P("dp", None, "dap"),
            P("dp", "dap", None, None),
            P("dp", None, "dap", None),
            P(),
            P(),
            P(),
            P(("dp", "dap"), None),
            P(("dp", "dap"), None),
            P(("dp", "dap"), None),
            P(("dp", "dap"), None),
        ),
        out_specs=(
            P(),
            P(),
            P(),
            P(),
            P(("dp", "dap"), None),
            P(("dp", "dap"), None),
            P(("dp", "dap"), None),
            P(("dp", "dap"), None),
        ),
        check_vma=False,
    )
```

```python
import jax
import jax.numpy as jnp
from jax import lax
from jax.experimental import pallas as pl
from jax.experimental.pallas import tpu as pltpu
from jax.sharding import PartitionSpec as P

FEATURE_WIDTH = 256
OUTER_LATENT = 32
SYMBOL_KINDS = 23
STEP = 10
PARAMS = 154048
ROWS = 1208
KINDS = 24
MASKED = 24.0
DEPTH = 128
RES = 16
LENGTH = 256
PLANE = 32
RINGS = 8
CROP = 16

PAIR_ROWS = 2 * KINDS
PAIR_BLOCKS = KINDS // 2
WIDE_ROWS = 32
BLOCKS = PAIR_BLOCKS + 2
CHUNKS = 4

beta_first = 0.9
beta_second = 0.999
adam_eps = 1e-06
learn_rate = 0.001
clip_norm = 0.1
norm_eps = 1e-05
ROOT_FLOOR = 1e-36

MESH = pl.DeviceIdType.MESH
F32 = jnp.float32
BF16 = jnp.bfloat16
F8 = jnp.float8_e4m3fn


def ring_hops(step, size):
    return min(step, size - step)


PLANE_STEPS = sorted(
    (-ring_hops(dx, 4) - ring_hops(dy, 4), dx, dy, dc)
    for dx in range(4)
    for dy in range(4)
    for dc in range(2)
    if dx + dy + dc > 0
)
RING_STEPS = sorted(range(1, RINGS), key=lambda s: -ring_hops(s, RINGS))
CROP_STEPS = sorted(
    (-ring_hops(dz, RINGS) - 2 * dx, dx, dz)
    for dz in range(RINGS)
    for dx in range(2)
    if dz + dx > 0
)
STAGES = ((0, 8), (8, 12), (12, 16))


def iota(shape, axis):
    return lax.broadcasted_iota(jnp.int32, shape, axis)


def dot(a, b):
    return jnp.dot(a, b, preferred_element_type=F32)


def dot_nt(a, b):
    return lax.dot_general(a, b, (((1,), (1,)), ((), ())), preferred_element_type=F32)


def dot_tn(a, b):
    return lax.dot_general(a, b, (((0,), (0,)), ((), ())), preferred_element_type=F32)


def halves_f32(x):
    high = x.astype(BF16).astype(F32)
    return high, x - high


def kernel(
    tok_hbm,
    valid_hbm,
    pair_hbm,
    adj_hbm,
    w_hbm,
    rest_hbm,
    grad_ref,
    clip_ref,
    tok_v,
    valid_v,
    pair_near,
    pair_middle,
    pair_far,
    adj_v,
    w_v,
    rest_v,
    codes,
    counts_near,
    counts_middle,
    counts_far,
    pair_part,
    pair_recv,
    pair_ring,
    pair_total,
    wide_part,
    wide_recv,
    wide_ring,
    wide_total,
    outer_v,
    fold,
    shifted,
    wide,
    w_out_v,
    mixed,
    pair_rows,
    pair_turned,
    normed_twice,
    local_sem,
    block_sem,
    code_send,
    code_recv,
    plane_send,
    plane_recv,
    ring_send,
    ring_recv,
    all_send,
    all_recv,
):
    dp = lax.axis_index("dp")
    dap = lax.axis_index("dap")
    z = lax.div(dap, 2)
    x_hi = lax.rem(dap, 2)
    core = lax.rem(dp, 2)
    y = lax.rem(lax.div(dp, 2), 4)
    x = x_hi * 2 + lax.div(dp, 8)

    xs = [lax.rem(x + dx, 4) for dx in range(4)]
    xs = [(lax.rem(value, 2) * 8, lax.div(value, 2)) for value in xs]
    ys = [lax.rem(y + dy, 4) * 2 for dy in range(4)]
    cores = [lax.rem(core + dc, 2) for dc in range(2)]

    def in_plane(dx, dy, dc):
        low, high = xs[dx]
        return cores[dc] * 16 + low + ys[dy] + high, (low + ys[dy] + cores[dc], z * 2 + high)

    slot = in_plane(0, 0, 0)[0]
    peers = [in_plane(*step[1:]) for step in PLANE_STEPS]
    zs = [lax.rem(z + dz, RINGS) * 2 for dz in range(RINGS)]
    mates = [zs[dz] + (1 - x_hi if dx else x_hi) for _, dx, dz in CROP_STEPS]
    order = [dap] + mates[::-1]

    barrier = pltpu.get_barrier_semaphore()
    greetings = [(step[0], (dp, mate)) for step, mate in zip(CROP_STEPS, mates)]
    greetings += [(step[0], peer) for step, (_, peer) in zip(PLANE_STEPS, peers)]
    greetings = [device for _, device in sorted(greetings, key=lambda pair: pair[0])]
    for device in greetings:
        pl.semaphore_signal(barrier, inc=1, device_id=device, device_id_type=MESH)


    loads = []
    for n, (src, dst) in enumerate(
        (
            (tok_hbm, tok_v),
            (valid_hbm, valid_v),
            (w_hbm, w_v),
            (adj_hbm, adj_v),
            (rest_hbm, rest_v),
        )
    ):
        copy = pltpu.make_async_copy(src, dst, local_sem.at[n])
        copy.start()
        loads.append(copy)

    cotangents = (pair_near, pair_middle, pair_far)
    for stage, (start, stop) in enumerate(STAGES):
        for n in range(start, stop):
            copy = pltpu.make_async_copy(
                pair_hbm.at[:, order[n]],
                cotangents[stage].at[:, pl.ds((n - start) * RES, RES)],
                block_sem.at[n],
            )
            copy.start()
            loads.append(copy)

    loads[0].wait()
    loads[1].wait()
    tok = tok_v[...].astype(F32)
    own = jnp.where(valid_v[...] != 0, tok, MASKED)
    codes[dap] = own.astype(BF16)
    pl.semaphore_wait(barrier, CROP - 1 + PLANE - 1)

    def wait_all(ref, sem):
        pltpu.make_async_copy(ref, ref, sem).wait()

    for n in range(CROP - 1, 0, -1):
        pltpu.make_async_remote_copy(
            src_ref=codes.at[dap],
            dst_ref=codes.at[dap],
            send_sem=code_send,
            recv_sem=code_recv.at[[start <= n < stop for start, stop in STAGES].index(True)],
            device_id=(dp, order[n]),
            device_id_type=MESH,
        ).start()

    spread = (iota((RES, 128), 1) % RES == iota((RES, 128), 0)).astype(F32)
    tiled = dot_tn(tok, spread)
    tiled = jnp.where(iota((DEPTH, 128), 0) % 8 == iota((DEPTH, 128), 1) // RES, tiled, 0.0)
    gather = (iota((RES, DEPTH), 1) // 8 == iota((RES, DEPTH), 0)).astype(F32)
    flat = dot(gather, tiled)
    kind = iota((KINDS, 128), 0).astype(F32)
    hot = jnp.concatenate(
        [(flat[q : q + 1, :] == kind).astype(F32) for q in range(RES)], axis=1
    ).astype(BF16)
    loads[3].wait()
    feat = dot(hot, adj_v[...])
    loads[4].wait()
    rest = rest_v[...]
    square = jnp.sum((rest * rest).reshape(32, 8, 512), axis=0)
    square = square[:, :128] + square[:, 128:256] + square[:, 256:384] + square[:, 384:]
    for copy in loads[5:]:
        copy.wait()
    pair_sum = jnp.zeros((16, 128), F32)
    for cotangent in cotangents:
        rows = cotangent.shape[0] * cotangent.shape[1]
        pair_sum = pair_sum + dot(jnp.ones((16, rows), BF16), cotangent[...].reshape(rows, 128))
    wide_part[0] = jnp.concatenate([feat[:, :128], pair_sum[:8]], axis=0)
    wide_part[1] = jnp.concatenate([feat[:, 128:], square], axis=0)

    def owner_of(p):
        return ((p % 16 // 2) * 2 + p // 16, z * 2 + p % 2)

    def plane_copy(part, recv, block, target):
        return pltpu.make_async_remote_copy(
            src_ref=part.at[block],
            dst_ref=recv.at[slot],
            send_sem=plane_send.at[0 if part is pair_part else 1],
            recv_sem=plane_recv,
            device_id=owner_of(target),
            device_id_type=MESH,
        )

    def to_owners(part, recv, first):
        for block in range(part.shape[0]):

            @pl.when(slot != first + block)
            def _():
                plane_copy(part, recv, block, first + block).start()

    def owns_pair(then):
        pl.when(slot < PAIR_BLOCKS)(then)

    def owns_wide(then):
        pl.when((slot >= PAIR_BLOCKS) & (slot < BLOCKS))(then)

    to_owners(wide_part, wide_recv, PAIR_BLOCKS)

    low_lane = iota((1, 128), 1) < 64
    hot_own = jnp.concatenate(
        [(own[i : i + 1, :] == kind).astype(F32) for i in range(RES)], axis=0
    ).astype(F8)

    sums = jnp.zeros((KINDS * KINDS, 128), F32)
    for stage, (start, stop) in enumerate(STAGES):
        wait_all(codes.at[pl.ds(0, stop - max(start, 1))], code_recv.at[stage])
        every = jnp.concatenate([codes[block].astype(F32) for block in order[start:stop]], axis=0)
        every = jnp.transpose(every)
        size = (stop - start) * RES
        counts = (counts_near, counts_middle, counts_far)[stage]
        count = 256 // size
        for first in range(0, KINDS, count):
            hot_all = jnp.concatenate(
                [(every == float(v)).astype(F32) for v in range(first, first + count)], axis=1
            )
            all_pairs = dot(hot_own, hot_all.astype(F8))
            for p in range(first // 2, (first + count) // 2):
                if size == 128:
                    both = all_pairs.reshape(RES, KINDS, 256)
                    both = jnp.concatenate([both[:, :, :128], both[:, :, 128:]], axis=1)
                else:
                    start_lane = (p - first // 2) * 128
                    both = all_pairs[:, start_lane : start_lane + 128]
                    turned = pltpu.roll(both, 64, 1).reshape(RES // 2, 2, KINDS, 128)
                    both = both.reshape(RES // 2, 2, KINDS, 128)
                    both = jnp.concatenate(
                        [
                            jnp.where(low_lane, both[:, 0], turned[:, 1]),
                            jnp.where(low_lane, turned[:, 0], both[:, 1]),
                        ],
                        axis=1,
                    )
                both = both.astype(BF16)
                for i in range(both.shape[0]):
                    counts[p * PAIR_ROWS : (p + 1) * PAIR_ROWS, i * 128 : (i + 1) * 128] = both[i]
        sums = sums + dot(counts[...], cotangents[stage][...].reshape(RES * size, 128))
    pair_part[...] = sums.astype(BF16).reshape(PAIR_BLOCKS, PAIR_ROWS, 128)
    to_owners(pair_part, pair_recv, 0)

    loads[2].wait()
    weights = jnp.concatenate(
        [
            w_v[pl.ds(0, 153600)].reshape(1200, 128),
            jnp.concatenate(
                [w_v[pl.ds(153600, PARAMS - 153600)], jnp.zeros((ROWS * 128 - PARAMS,), F32)]
            ).reshape(8, 128),
        ],
        axis=0,
    )
    weights = weights.astype(BF16).astype(F32)
    shifted[0:ROWS] = pltpu.roll(weights, 64, 1)
    w_out_v[...] = jnp.where(
        low_lane, shifted[pl.ds(132, 1024), :], shifted[pl.ds(133, 1024), :]
    )
    first = jnp.where(
        low_lane,
        shifted[pl.ds(1157, KINDS, stride=2), :],
        shifted[pl.ds(1158, KINDS, stride=2), :],
    )
    second = jnp.where(
        low_lane,
        shifted[pl.ds(1158, KINDS, stride=2), :],
        shifted[pl.ds(1159, KINDS, stride=2), :],
    )
    table = jnp.concatenate([first, second], axis=1)
    table = jnp.where(iota((KINDS, FEATURE_WIDTH), 0) < SYMBOL_KINDS, table, 0.0)
    center = jnp.mean(table, axis=1, keepdims=True)
    variance = jnp.mean((table - center) ** 2, axis=1, keepdims=True)
    inverse = lax.rsqrt(variance + norm_eps)
    unit = (table - center) * inverse
    gain = jnp.concatenate([weights[0:1], weights[1:2]], axis=1)
    shift = jnp.concatenate([weights[2:3], weights[3:4]], axis=1)
    normed = (unit * gain + shift).astype(BF16).astype(F32)
    w_rows = weights[4:132]
    pair_rows[pl.ds(0, 128, stride=2), :] = jnp.where(low_lane, w_rows, 0.0)
    pair_rows[pl.ds(1, 128, stride=2), :] = jnp.where(low_lane, pltpu.roll(w_rows, 64, 1), 0.0)
    w_pair = pair_rows[...]
    pair_turned[...] = jnp.transpose(w_pair).astype(BF16)
    bias = jnp.where(low_lane, weights[132:133], 0.0)
    acts = (dot(normed, w_pair) + bias).astype(BF16).astype(F32)
    acts = jnp.where(iota((KINDS, 128), 0) < SYMBOL_KINDS, acts, 0.0)

    normed_twice[...] = jnp.transpose(jnp.concatenate([normed, normed], axis=0)).astype(BF16)

    he_row = iota((1024, 128), 0)
    lane = iota((1024, 128), 1)
    acts_t = jnp.transpose(acts).astype(BF16)
    left_of = dot((he_row // 32 == lane).astype(F32).astype(BF16), acts_t).astype(BF16)
    right_of = dot((he_row % 32 == lane - 32).astype(F32).astype(BF16), acts_t).astype(BF16)
    uv = iota((KINDS, KINDS * KINDS), 1)
    kind_row = iota((KINDS, KINDS * KINDS), 0)
    outer = dot(left_of, (uv % KINDS == kind_row).astype(F32).astype(BF16)) * (1.0 / DEPTH)
    outer = outer * dot(right_of, (uv // KINDS == kind_row).astype(F32).astype(BF16))
    outer_v[...] = outer.astype(BF16)

    def mix(weights, blocks):
        blocks = jnp.concatenate(blocks, axis=1).astype(BF16)
        mixes = dot(weights.astype(BF16), blocks) * (1.0 / DEPTH)
        for h in range(OUTER_LATENT):
            mixed[pl.ds(h, KINDS, stride=32), :] = mixes[:, h * 128 : (h + 1) * 128]
        turned = jnp.concatenate([mixed[v * 32 : (v + 1) * 32] for v in range(KINDS)], axis=1)
        return halves_f32(turned)

    mixes = mix(
        acts[:, OUTER_LATENT : 2 * OUTER_LATENT],
        [w_out_v[h * 32 : (h + 1) * 32] for h in range(OUTER_LATENT)],
    ) + mix(
        acts[:, :OUTER_LATENT],
        [w_out_v[pl.ds(e, 32, stride=32), :] for e in range(OUTER_LATENT)],
    )
    fold[...] = jnp.transpose(jnp.concatenate(mixes, axis=0)).astype(BF16)

    def reduce(block, part, recv, ring, total, others):
        recv[slot] = part[block]
        wait_all(recv.at[pl.ds(0, PLANE - 1)], plane_recv)
        ring[z] = jnp.sum(recv[...].astype(F32), axis=0).astype(ring.dtype)
        for step in RING_STEPS:
            pltpu.make_async_remote_copy(
                src_ref=ring.at[z],
                dst_ref=ring.at[z],
                send_sem=ring_send,
                recv_sem=ring_recv,
                device_id=(dp, zs[step] + x_hi),
                device_id_type=MESH,
            ).start()
        wait_all(ring.at[pl.ds(0, RINGS - 1)], ring_recv)
        total[block] = jnp.sum(ring[...].astype(F32), axis=0).astype(total.dtype)
        for _, peer in peers:
            pltpu.make_async_remote_copy(
                src_ref=total.at[block],
                dst_ref=total.at[block],
                send_sem=all_send,
                recv_sem=all_recv.at[others],
                device_id=peer,
                device_id_type=MESH,
            ).start()

    @owns_pair
    def _():
        reduce(slot, pair_part, pair_recv, pair_ring, pair_total, 0)
        wait_all(pair_total.at[pl.ds(0, PAIR_BLOCKS - 1)], all_recv.at[0])
        wait_all(wide_total, all_recv.at[1])

    @owns_wide
    def _():
        reduce(slot - PAIR_BLOCKS, wide_part, wide_recv, wide_ring, wide_total, 1)
        wait_all(pair_total, all_recv.at[0])
        wait_all(wide_total.at[pl.ds(0, 1)], all_recv.at[1])

    @pl.when(slot >= BLOCKS)
    def _():
        wait_all(pair_total, all_recv.at[0])
        wait_all(wide_total, all_recv.at[1])

    summed = pair_total[...].reshape(KINDS * KINDS, 128)
    mixed[0 : KINDS * KINDS] = summed.astype(F32)
    by_first = jnp.concatenate([mixed[v * KINDS : (v + 1) * KINDS] for v in range(KINDS)], axis=1)
    by_second = jnp.concatenate(
        [mixed[pl.ds(u, KINDS, stride=KINDS), :] for u in range(KINDS)], axis=1
    )
    act = dot(jnp.concatenate([by_first, by_second], axis=0).astype(BF16), fold[...])
    act = jnp.where(low_lane, act[:KINDS], act[KINDS:])
    act = act + pltpu.roll(act, 96, 1)
    act = jnp.where(iota((1, 128), 1) < OUTER_LATENT, act, pltpu.roll(act, 96, 1))
    act = jnp.where((iota((KINDS, 128), 0) < SYMBOL_KINDS) & low_lane, act, 0.0)
    w_out_grad = dot(outer_v[...], pltpu.roll(mixed[0 : KINDS * KINDS], 64, 1).astype(BF16))
    act_parts = jnp.concatenate(halves_f32(act), axis=0)
    act_parts = act_parts.astype(BF16)
    norm_grad = dot(act_parts, pair_turned[...])
    norm_grad = norm_grad[:KINDS] + norm_grad[KINDS:]
    wide[...] = dot(normed_twice[...], act_parts)
    w_pair_grad = wide[pl.ds(0, 128, stride=2), :] + pltpu.roll(
        wide[pl.ds(1, 128, stride=2), :], 64, 1
    )
    gained = norm_grad * gain
    feat = jnp.concatenate([wide_total[0][:KINDS], wide_total[1][:KINDS]], axis=1)
    table_grad = feat + inverse * (
        gained
        - jnp.mean(gained, axis=1, keepdims=True)
        - unit * jnp.mean(gained * unit, axis=1, keepdims=True)
    )
    gain_grad = jnp.sum(norm_grad * unit, axis=0, keepdims=True)
    shift_grad = jnp.sum(norm_grad, axis=0, keepdims=True)
    bias_grad = jnp.sum(act, axis=0, keepdims=True)

    shifted[0:8] = jnp.zeros((8, 128), F32)
    shifted[8:1032] = w_out_grad
    shifted[1032:1088] = jnp.zeros((56, 128), F32)
    shifted[1032:1033] = pltpu.roll(wide_total[0][KINDS : KINDS + 1], 64, 1)
    shifted[pl.ds(1033, SYMBOL_KINDS, stride=2), :] = pltpu.roll(
        table_grad[:SYMBOL_KINDS, :128], 64, 1
    )
    shifted[pl.ds(1034, SYMBOL_KINDS, stride=2), :] = pltpu.roll(
        table_grad[:SYMBOL_KINDS, 128:], 64, 1
    )
    grad_ref[128:ROWS] = jnp.where(low_lane, shifted[3:1083], shifted[4:1084])
    grad_ref[0:4] = jnp.concatenate(
        [gain_grad[:, :128], gain_grad[:, 128:], shift_grad[:, :128], shift_grad[:, 128:]], axis=0
    )
    grad_ref[4:132] = w_pair_grad
    grad_ref[132:133] = jnp.where(low_lane, bias_grad, grad_ref[132:133])
    pair_sum = wide_total[0][KINDS : KINDS + 1]
    single = gain_grad * gain_grad + shift_grad * shift_grad
    single = single[:, :128] + single[:, 128:] + bias_grad * bias_grad + pair_sum * pair_sum
    by_kind = jnp.where(iota((KINDS, FEATURE_WIDTH), 0) < SYMBOL_KINDS, table_grad, 0.0)
    by_kind = jnp.sum((by_kind * by_kind).reshape(KINDS // 8, 8, FEATURE_WIDTH), axis=0)
    squares = (
        jnp.sum((w_out_grad * w_out_grad).reshape(128, 8, 128), axis=0)
        + jnp.sum((w_pair_grad * w_pair_grad).reshape(16, 8, 128), axis=0)
        + by_kind[:, :128]
        + by_kind[:, 128:]
        + wide_total[1][KINDS:]
        + jnp.where(iota((8, 128), 0) == 0, single, 0.0)
    )
    norm = jnp.sum(squares)
    norm = jnp.sqrt(jnp.full((1, 512), norm, F32))
    clip_ref[...] = jnp.minimum(1.0, clip_norm / (norm + 1e-06))

    wait_all(codes.at[pl.ds(0, CROP - 1)], code_send)

    def finish(recv, ring, pairs, wides):
        wait_all(pair_part.at[pl.ds(0, pairs)], plane_send.at[0])
        wait_all(wide_part.at[pl.ds(0, wides)], plane_send.at[1])
        if recv is not None:
            wait_all(ring.at[pl.ds(0, RINGS - 1)], ring_send)
            wait_all(recv.at[pl.ds(0, PLANE - 1)], all_send)

    @owns_pair
    def _():
        finish(pair_recv, pair_ring, PAIR_BLOCKS - 1, 2)

    @owns_wide
    def _():
        finish(wide_recv, wide_ring, PAIR_BLOCKS, 1)

    @pl.when(slot >= BLOCKS)
    def _():
        finish(None, None, PAIR_BLOCKS, 2)


def in_hbm(array):
    return pltpu.with_memory_space_constraint(array, pltpu.HBM)


def gradients(*arrays):
    return pl.pallas_call(
        kernel,
        out_shape=(
            jax.ShapeDtypeStruct((ROWS, 128), F32),
            jax.ShapeDtypeStruct((1, 512), F32),
        ),
        in_specs=[pl.BlockSpec(memory_space=pltpu.HBM)] * 6,
        out_specs=(
            pl.BlockSpec(memory_space=pltpu.VMEM),
            pl.BlockSpec(memory_space=pltpu.VMEM),
        ),
        scratch_shapes=[
            pltpu.VMEM((RES, DEPTH), jnp.int32),
            pltpu.VMEM((RES, DEPTH), jnp.int32),
            pltpu.VMEM((RES, 128, 128), BF16),
            pltpu.VMEM((RES, 64, 128), BF16),
            pltpu.VMEM((RES, 64, 128), BF16),
            pltpu.VMEM((DEPTH * RES, FEATURE_WIDTH), BF16),
            pltpu.VMEM((PARAMS,), F32),
            pltpu.VMEM((256, 512), F32),
            pltpu.VMEM((CROP, RES, DEPTH), BF16),
            pltpu.VMEM((KINDS * KINDS, RES * 128), BF16),
            pltpu.VMEM((KINDS * KINDS, RES * 64), BF16),
            pltpu.VMEM((KINDS * KINDS, RES * 64), BF16),
            pltpu.VMEM((PAIR_BLOCKS, PAIR_ROWS, 128), BF16),
            pltpu.VMEM((PLANE, PAIR_ROWS, 128), BF16),
            pltpu.VMEM((RINGS, PAIR_ROWS, 128), BF16),
            pltpu.VMEM((PAIR_BLOCKS, PAIR_ROWS, 128), BF16),
            pltpu.VMEM((2, WIDE_ROWS, 128), F32),
            pltpu.VMEM((PLANE, WIDE_ROWS, 128), F32),
            pltpu.VMEM((RINGS, WIDE_ROWS, 128), F32),
            pltpu.VMEM((2, WIDE_ROWS, 128), F32),
            pltpu.VMEM((1024, KINDS * KINDS), BF16),
            pltpu.VMEM((KINDS * 128, 128), BF16),
            pltpu.VMEM((ROWS + 8, 128), F32),
            pltpu.VMEM((FEATURE_WIDTH, 128), F32),
            pltpu.VMEM((1024, 128), F32),
            pltpu.VMEM((KINDS * 32, 128), F32),
            pltpu.VMEM((FEATURE_WIDTH, 128), F32),
            pltpu.VMEM((128, FEATURE_WIDTH), BF16),
            pltpu.VMEM((FEATURE_WIDTH, 2 * KINDS), BF16),
            pltpu.SemaphoreType.DMA((5,)),
            pltpu.SemaphoreType.DMA((CROP,)),
            pltpu.SemaphoreType.DMA,
            pltpu.SemaphoreType.DMA((len(STAGES),)),
            pltpu.SemaphoreType.DMA((2,)),
            pltpu.SemaphoreType.DMA,
            pltpu.SemaphoreType.DMA,
            pltpu.SemaphoreType.DMA,
            pltpu.SemaphoreType.DMA,
            pltpu.SemaphoreType.DMA((2,)),
        ],
        compiler_params=pltpu.CompilerParams(
            collective_id=0, has_side_effects=True, vmem_limit_bytes=40 * 1024 * 1024
        ),
        cost_estimate=pl.CostEstimate(
            flops=3_000_000_000, bytes_accessed=40_000_000, transcendentals=0
        ),
    )(*[in_hbm(array) for array in arrays])


def adam_update(master, moment_one, moment_two, scaled):
    first = beta_first * moment_one + (1.0 - beta_first) * scaled
    second = beta_second * moment_two + (1.0 - beta_second) * scaled * scaled
    fix_first = 1.0 - beta_first**STEP
    fix_second = 1.0 - beta_second**STEP
    root = second * lax.rsqrt(jnp.maximum(second, ROOT_FLOOR)) * fix_second**-0.5
    size = root + adam_eps
    guess = pl.reciprocal(size, approx=True)
    guess = guess * (2.0 - size * guess)
    return (master - first * (learn_rate / fix_first) * guess, first, second)


def update_kernel(
    grad_ref,
    clip_ref,
    master_ref,
    one_ref,
    two_ref,
    rest_grad_ref,
    rest_master_ref,
    rest_one_ref,
    rest_two_ref,
    *refs,
):
    outs, held, sems = refs[:8], refs[8:16], refs[16]
    clip = clip_ref[...]
    rest_step = rest_grad_ref.shape[0] // CHUNKS
    flat_step = 1024 * 38
    copies = []

    def send(n, where):
        copy = pltpu.make_async_copy(held[n].at[where], outs[n].at[where], sems.at[len(copies)])
        copy.start()
        copies.append(copy)

    for chunk in range(CHUNKS):
        where = pl.ds(chunk * rest_step, rest_step)
        new = adam_update(
            rest_master_ref[where], rest_one_ref[where], rest_two_ref[where], rest_grad_ref[where] * clip
        )
        for n, value in enumerate(new + (new[0],)):
            held[4 + n][where] = value.astype(held[4 + n].dtype)
            send(4 + n, where)
    factor = jnp.max(clip)
    for chunk in range(CHUNKS):
        start = chunk * flat_step
        where = pl.ds(start, min(flat_step, PARAMS - start))
        new = adam_update(master_ref[where], one_ref[where], two_ref[where], grad_ref[where] * factor)
        for n, value in enumerate(new + (new[0],)):
            held[n][where] = value.astype(held[n].dtype)
            send(n, where)
    for copy in copies:
        copy.wait()


def updates(grad, clip, master, one, two, rest_grad, rest_master, rest_one, rest_two):
    flat = [jax.ShapeDtypeStruct(master.shape, dtype) for dtype in (F32, F32, F32, BF16)]
    rows = [jax.ShapeDtypeStruct(rest_master.shape, dtype) for dtype in (F32, F32, F32, BF16)]
    return pl.pallas_call(
        update_kernel,
        out_shape=tuple(flat + rows),
        in_specs=[pl.BlockSpec(memory_space=pltpu.VMEM)] * 9,
        out_specs=tuple([pl.BlockSpec(memory_space=pltpu.HBM)] * 8),
        scratch_shapes=[pltpu.VMEM(out.shape, out.dtype) for out in flat + rows]
        + [pltpu.SemaphoreType.DMA((8 * CHUNKS,))],
        compiler_params=pltpu.CompilerParams(vmem_limit_bytes=20 * 1024 * 1024),
        cost_estimate=pl.CostEstimate(
            flops=5_000_000, bytes_accessed=8_000_000, transcendentals=0
        ),
    )(grad, clip, master, one, two, rest_grad, rest_master, rest_one, rest_two)


def shards(
    symbol_codes,
    aligned_validity,
    pair_update_cotangent,
    aligned_feature_adjoint,
    local_master_weights,
    local_first_moment,
    local_second_moment,
    remaining_master_weights,
    remaining_first_moment,
    remaining_second_moment,
    remaining_gradient,
):
    gradient, clip = gradients(
        jnp.transpose(symbol_codes[0]),
        jnp.transpose(aligned_validity[0]),
        pair_update_cotangent.reshape(RES, CROP, RES, 128),
        aligned_feature_adjoint.reshape(DEPTH * RES, FEATURE_WIDTH),
        local_master_weights,
        remaining_gradient,
    )
    return updates(
        gradient.reshape(-1),
        clip,
        local_master_weights,
        local_first_moment,
        local_second_moment,
        remaining_gradient,
        remaining_master_weights,
        remaining_first_moment,
        remaining_second_moment,
    )


def solution(mesh):
    return jax.shard_map(
        shards,
        mesh=mesh,
        in_specs=(
            P("dp", None, "dap"),
            P("dp", None, "dap"),
            P("dp", "dap", None, None),
            P("dp", None, "dap", None),
            P(),
            P(),
            P(),
            P(("dp", "dap"), None),
            P(("dp", "dap"), None),
            P(("dp", "dap"), None),
            P(("dp", "dap"), None),
        ),
        out_specs=(
            P(),
            P(),
            P(),
            P(),
            P(("dp", "dap"), None),
            P(("dp", "dap"), None),
            P(("dp", "dap"), None),
            P(("dp", "dap"), None),
        ),
        check_vma=False,
    )
```
